32 devices in a mesh: groups: 2 (over x), dev: 16 (over z, y, core).
Axes of the slice: x: 2, y: 2, z: 4, core: 2. Of those that a mesh axis runs over, the one named last changes fastest.
Arguments:
- queries: bfloat16 [2, 32, 128, 1024], P(None, ('groups', 'dev')), parts along dimension 1, may hold values from -180 to 180
- keys_values: bfloat16 [2, 32, 2, 1664, 128], P(None, ('groups', 'dev')), parts along dimension 1, may hold values from -6 to 6
- residual: bfloat16 [2, 2048, 2048], P(None, ('groups', 'dev')), parts along dimension 1, may hold values from -6 to 6
- norm_gain: float32 [2048], replicated, may hold values from 0.1 to 1.9
- gate_up: bfloat16 [16, 2048, 1536], P('dev'), may hold values from -0.125 to 0.125
- down_proj: bfloat16 [16, 768, 2048], P('dev'), may hold values from -0.21875 to 0.21875
- expert_ids: int32 [2, 2048, 8], P(None, ('groups', 'dev')), parts along dimension 1, may hold values from 0 to 15, all different within a row; in each aligned block of 64 rows (0 to 63, 64 to 127, ..., all dimensions but the last counted through in order) at most 40 rows name the same one
- expert_gates: int32 [2, 2048, 8], P(None, ('groups', 'dev')), parts along dimension 1, may hold values from 1 to 1023
Outputs:
- layer_out: bfloat16 [2, 2048, 2048], P(None, ('groups', 'dev')), parts along dimension 1
The draws below stay inside these ranges and needn't reach their ends.
There are 2 independent parts, one for each index of `groups`. The reference program is written for one: setup_inputs(seed, part) draws one part's arguments, and reference() takes and returns one part's arrays. A program takes and returns all parts, laid end to end along the dimension named above; an argument that names none is the same for every part. Nothing has to cross between parts.
Inputs may be any that keep to these rules, and one draw needn't show every extreme that they name: `expert_ids`: in each micro-batch and each aligned block of 64 rows (the tokens of one device), no expert is named by more than 40 rows, a bound that some block reaches; the 8 experts of a row differ.
All inputs are finite; a program needn't handle non-finite values.
Results may differ from the reference program's by a relative error of at most 0.0039.
Values may be sent and summed in bfloat16 or wider, within the bound.
No kernel may reach another device: no remote copies, remote signals or barrier semaphores. Data moves between devices by JAX's collectives and lax.ppermute only.
A program may use at most 128 MiB of HBM per device.

```python
import math
import jax
import jax.numpy as jnp
import numpy as np
from jax import lax

D = 2048
FF = 768
HD = 128
GQ = 8
KVH = 2
TOPK = 8
MB = 2
SPAN = 128
SEQS = 8
UNITS = 16
CTX = 1664
TOK_DEV = 64
TOKENS = 1024
EXPERTS = 16
CAP = 40
N_DEV = 16


def joint_draw(key):
    seed_pairs = jax.random.fold_in(key, 101)
    seed_query = jax.random.fold_in(key, 202)
    cached_pairs = jnp.clip(jax.random.normal(seed_pairs, (MB, UNITS, 2, CTX, HD), jnp.float32), -6.0, 6.0)
    query_rows = jnp.clip(2.0 * jax.random.normal(seed_query, (MB, UNITS, SPAN, GQ * HD), jnp.float32), -12.0, 12.0)
    return (cached_pairs, query_rows)


def draw_queries(key, part):
    return joint_draw(key)[1].astype(jnp.bfloat16)


def draw_keys_values(key, part):
    return joint_draw(key)[0].astype(jnp.bfloat16)


def plant(result, key, smallest, top_value):
    longest = result.shape.index(max(result.shape))
    spots = []
    for shift in (0, 1):
        where = [jax.random.randint(jax.random.fold_in(key, axis), (), 0, length) for axis, length in enumerate(result.shape)]
        where[longest] = (where[longest] + shift) % result.shape[longest]
        spots.append(tuple(where))
    return result.at[spots[0]].set(smallest).at[spots[1]].set(top_value)


def block_levels(key, dims, cuts, smallest, high):
    level, own = 1.0, jax.random.fold_in(key, 6)
    for axis_at, parts in cuts:
        draws = jnp.exp(jax.random.uniform(jax.random.fold_in(own, axis_at), (parts,), jnp.float32, smallest / len(cuts), high / len(cuts)))
        level = level * jnp.repeat(draws, dims[axis_at] // parts).reshape([-1 if axis == axis_at else 1 for axis in range(len(dims))])
    return level


def routed_block(key, own, number, rows, number_of, top, most, skew):
    order = jax.random.permutation(key, number_of)
    crowded, ordinary = load_shares(number_of, rows * top, most, skew, True), load_shares(number_of, rows * top, most, skew, False)
    places = jnp.arange(number_of)

    def named(lengths, offset_by):
        used = int((lengths > 0).sum())
        fixed = max(1, used // 4)
        shifted = fixed + (places - fixed + offset_by * (used - fixed)) % max(1, number_of - fixed)
        return jnp.zeros((number_of,), jnp.int32).at[order[jnp.where(places < fixed, places, shifted)]].set(jnp.asarray(lengths, jnp.int32))

    lengths = jnp.where(number % 4 == 0, named(crowded, number // 4), named(ordinary, number - number // 4 - 1))
    mixed = jax.random.permutation(jax.random.fold_in(own, 3), number_of)
    giver, receiver = mixed[0:number_of // 2 * 2:2], mixed[1:number_of // 2 * 2:2]
    slack = jnp.minimum(lengths[giver] - 1, most - lengths[receiver]) // 2
    slack = jnp.where((giver == order[0]) | (receiver == order[0]) | (lengths[receiver] == 0), 0, jnp.maximum(slack, 0))
    shifted = jax.random.randint(jax.random.fold_in(own, 4), (number_of // 2,), 0, 1 << 20) % (slack + 1)
    lengths = lengths.at[giver].add(-shifted).at[receiver].add(shifted)
    labels = jnp.searchsorted(jnp.cumsum(lengths), jnp.arange(rows * top), side="right").astype(jnp.int32)
    table = labels.reshape(top, rows).T
    table = table[jax.random.permutation(jax.random.fold_in(own, 1), rows)]
    offset_by = jax.random.randint(jax.random.fold_in(own, 2), (rows, 1), 0, top)
    return jnp.take_along_axis(table, (jnp.arange(top)[None, :] + offset_by) % top, axis=1)


def load_shares(number_of, total, most, slope, full):
    portions = [(1 << 20) // math.isqrt(rank ** slope) + 1 for rank in range(1, number_of + 1)]
    largest = most if full else min(most, max(-(-total // number_of), total * portions[0] // sum(portions)))
    least = 1 if total - largest >= number_of - 1 else 0
    counts, spare = [largest] + [least] * (number_of - 1), total - largest - least * (number_of - 1)
    while spare > 0:
        free = [i for i in range(1, number_of) if counts[i] < largest] or [i for i in range(1, number_of) if counts[i] < most]
        whole, remaining = sum([portions[i] for i in free]), spare
        for i in free:
            extra = min(most - counts[i], max(1, remaining * portions[i] // whole), spare)
            counts[i] = counts[i] + extra
            spare = spare - extra
    return np.array(counts)


def centred(stream_key, extent, width, limit, shards=(), kind=jnp.bfloat16):
    values = width * jax.random.normal(stream_key, extent, jnp.float32)
    if shards:
        values = values * block_levels(stream_key, extent, shards, -0.22, 0.18)
    return jnp.clip(values, -limit, limit).astype(kind)


def setup_inputs(seed: int = 0, part: int = 0) -> dict:
    streams_of = jax.random.split(jax.random.key(seed), 9)
    part_splits = jax.random.split(jax.random.fold_in(streams_of[8], part), 9)
    queries = draw_queries(jax.random.fold_in(jax.random.fold_in(streams_of[8], part), 71), part)
    keys_values = draw_keys_values(jax.random.fold_in(jax.random.fold_in(streams_of[8], part), 71), part)
    residual = centred(part_splits[2], (MB, TOKENS, D), 1.0, 6.0, ((1, 16),))
    norm_gain = jnp.clip(1.0 + 0.18 * jax.random.normal(streams_of[3], (D,), jnp.float32), 0.1, 1.9)
    gate_up = centred(streams_of[4], (EXPERTS, D, 2 * FF), D ** -0.5, 0.125, ((0, 16),))
    down_proj = centred(streams_of[5], (EXPERTS, FF, D), FF ** -0.5, 0.21875, ((0, 16),))
    expert_ids_keys = jax.random.split(jax.random.fold_in(part_splits[6], 1), MB * TOKENS // TOK_DEV)
    expert_ids_turns = jax.random.permutation(jax.random.fold_in(part_splits[6], 3), MB * TOKENS // TOK_DEV)
    expert_ids = jax.vmap(lambda own, number: routed_block(jax.random.fold_in(part_splits[6], 2), own, number, TOK_DEV, EXPERTS, TOPK, CAP, 1))(expert_ids_keys, expert_ids_turns).reshape((MB, TOKENS, TOPK))
    expert_gates = plant(jax.random.randint(part_splits[7], (MB, TOKENS, TOPK), 1, 1024), jax.random.fold_in(part_splits[7], 1), 1, 1023).astype(jnp.int32)
    return {"queries": queries, "keys_values": keys_values, "residual": residual, "norm_gain": norm_gain, "gate_up": gate_up, "down_proj": down_proj, "expert_ids": expert_ids, "expert_gates": expert_gates}


def attend(query_rows, cached_pairs):
    batches, length, feat_width = query_rows.shape
    context = cached_pairs.shape[2]
    head_size = cached_pairs.shape[3]
    groups = feat_width // head_size
    head_rows = query_rows.reshape(batches, length, groups, head_size).astype(jnp.float32)
    scores = jnp.einsum('mqgd,mkd->mgqk', head_rows, cached_pairs[:, 0].astype(jnp.float32)) / math.sqrt(head_size)
    query_pos = context - length + lax.broadcasted_iota(jnp.int32, (length, context), 0)
    key_pos = lax.broadcasted_iota(jnp.int32, (length, context), 1)
    allowed = key_pos <= query_pos
    scores = jnp.where(allowed, scores, -1e+30)
    highest = lax.optimization_barrier(jnp.max(scores, axis=-1, keepdims=True))
    scaled_exp = jnp.where(allowed, jnp.exp(scores - highest), 0.0)
    totals = lax.optimization_barrier(jnp.sum(scaled_exp, axis=-1, keepdims=True))
    weights = (scaled_exp / totals).astype(jnp.bfloat16)
    blended = jnp.einsum('mgqk,mkd->mqgd', weights.astype(jnp.float32), cached_pairs[:, 1].astype(jnp.float32))
    return blended.astype(jnp.bfloat16).reshape(batches, length, feat_width)

def reference(queries, keys_values, residual, norm_gain, gate_up, down_proj, expert_ids, expert_gates):
    unit_first = (jnp.moveaxis(queries, 1, 0), jnp.moveaxis(keys_values, 1, 0))
    blended_heads = lax.map(lambda unit_pair: attend(unit_pair[0], unit_pair[1]), unit_first)
    grouped = blended_heads.reshape(SEQS, KVH, MB, N_DEV, SPAN // N_DEV, GQ * HD)
    attn_rows = jnp.transpose(grouped, (2, 3, 0, 4, 1, 5)).reshape(MB, TOKENS, D)
    stream = residual.astype(jnp.float32) + attn_rows.astype(jnp.float32)
    meansq = lax.optimization_barrier(jnp.mean(stream * stream, axis=-1, keepdims=True))
    normed = (stream * lax.rsqrt(meansq + 1e-06) * norm_gain).astype(jnp.bfloat16)
    shares = expert_gates.astype(jnp.float32)
    shares = shares / lax.optimization_barrier(jnp.sum(shares, axis=-1, keepdims=True))
    flat_ids = expert_ids.reshape(MB, N_DEV, TOK_DEV * TOPK)
    one_hot = (flat_ids[..., None] == jnp.arange(EXPERTS, dtype=jnp.int32)).astype(jnp.int32)
    ranking = lax.optimization_barrier(jnp.sum((jnp.cumsum(one_hot, axis=2) - one_hot) * one_hot, axis=-1)).astype(jnp.int32)
    batch_ids = lax.broadcasted_iota(jnp.int32, flat_ids.shape, 0)
    source_ids = lax.broadcasted_iota(jnp.int32, flat_ids.shape, 1)
    entry_ids = lax.broadcasted_iota(jnp.int32, flat_ids.shape, 2)
    token_rows = (batch_ids * TOKENS + source_ids * TOK_DEV + entry_ids // TOPK).astype(jnp.int32)
    row_table = jnp.zeros((EXPERTS, MB, N_DEV, CAP), jnp.int32).at[flat_ids, batch_ids, source_ids, ranking].set(token_rows)
    share_table = jnp.zeros((EXPERTS, MB, N_DEV, CAP), jnp.float32).at[flat_ids, batch_ids, source_ids, ranking].set(shares.reshape(MB, N_DEV, TOK_DEV * TOPK))
    flat_normed = normed.reshape(MB * TOKENS, D)

    def expert_turn(running, inputs):
        row_ids, share_ids, gate_mat, down_mat = inputs
        index_list = row_ids.reshape(-1)
        rows_in = flat_normed[index_list]
        projected = jnp.dot(rows_in, gate_mat, preferred_element_type=jnp.float32)
        hidden = (jax.nn.silu(projected[:, :FF]) * projected[:, FF:]).astype(jnp.bfloat16)
        output = jnp.dot(hidden, down_mat, preferred_element_type=jnp.float32).astype(jnp.bfloat16)
        running = running.at[index_list].add(share_ids.reshape(-1, 1) * output.astype(jnp.float32))
        return (running, None)
    start_sum = jnp.zeros((MB * TOKENS, D), jnp.float32)
    mixture, ignored = lax.scan(expert_turn, start_sum, (row_table, share_table, gate_up, down_proj))
    return (stream + mixture.reshape(MB, TOKENS, D)).astype(jnp.bfloat16)
```

```python
import functools
import math

import jax
import jax.numpy as jnp
from jax import lax
from jax.experimental import pallas as pl
from jax.experimental.pallas import tpu as pltpu
from jax.sharding import PartitionSpec as P

F32 = jnp.float32
BF16 = jnp.bfloat16


def attend_kernel(q_ref, kv_ref, out_ref):
    length, feat_width = q_ref.shape
    context, head_size = kv_ref.shape[1:]
    scale = math.log2(math.e) / math.sqrt(head_size)
    keys, values = kv_ref[0], kv_ref[1]
    row = lax.broadcasted_iota(jnp.int32, (length, length), 0)
    col = lax.broadcasted_iota(jnp.int32, (length, length), 1)
    allowed = col <= row
    for head in range(feat_width // head_size):
        cols = slice(head * head_size, (head + 1) * head_size)
        scores = lax.dot_general(
            q_ref[:, cols], keys, (((1,), (1,)), ((), ())), preferred_element_type=F32
        )
        cached = scores[:, : context - length]
        fresh = jnp.where(allowed, scores[:, context - length :], -1e30)
        highest = jnp.maximum(
            jnp.max(cached, axis=-1, keepdims=True), jnp.max(fresh, axis=-1, keepdims=True)
        )
        grown = jnp.concatenate(
            [jnp.exp2((cached - highest) * scale), jnp.exp2((fresh - highest) * scale)], axis=1
        )
        total = jnp.sum(grown, axis=-1, keepdims=True)
        blended = jnp.dot(grown.astype(BF16), values, preferred_element_type=F32)
        out_ref[:, cols] = (blended / total).astype(BF16)


def attend(queries, keys_values, batch):
    length, feat_width = queries.shape[2:]
    context, head_size = keys_values.shape[3:]
    pairs = length * (feat_width // head_size) * context
    return pl.pallas_call(
        attend_kernel,
        out_shape=jax.ShapeDtypeStruct((length, feat_width), BF16),
        grid=(1,),
        in_specs=[
            pl.BlockSpec((None, None, length, feat_width), lambda i: (batch, 0, 0, 0)),
            pl.BlockSpec((None, None, 2, context, head_size), lambda i: (batch, 0, 0, 0, 0)),
        ],
        out_specs=pl.BlockSpec((length, feat_width), lambda i: (0, 0)),
        compiler_params=pltpu.CompilerParams(vmem_limit_bytes=32 << 20),
        cost_estimate=pl.CostEstimate(
            flops=4 * pairs * head_size,
            bytes_accessed=2 * (2 * length * feat_width + 2 * context * head_size),
            transcendentals=pairs,
        ),
        name="attend",
    )(queries, keys_values)


def expert_kernel(me_ref, x_ref, share_ref, gate_ref, up_ref, down_ref, mine_ref, other_ref, hidden_ref, *, steps, offset):
    step = pl.program_id(0)
    rows = x_ref.shape[0]
    tokens = rows // share_ref.shape[0]
    lanes = share_ref.shape[2]

    @pl.when(step < steps)
    def _():
        x = x_ref[...]
        gate = jnp.dot(x, gate_ref[...], preferred_element_type=F32)
        up = jnp.dot(x, up_ref[...], preferred_element_type=F32)
        hidden_ref[step] = (gate / (1.0 + jnp.exp(-gate)) * up).astype(BF16)

    @pl.when(step >= steps)
    def _():
        width = hidden_ref.shape[2]
        total = jnp.dot(hidden_ref[0], down_ref[:width], preferred_element_type=F32)
        for part in range(1, steps):
            total += jnp.dot(
                hidden_ref[part],
                down_ref[part * width : (part + 1) * width],
                preferred_element_type=F32,
            )
        token = lax.broadcasted_iota(jnp.int32, (tokens, lanes), 0)
        lane = lax.broadcasted_iota(jnp.int32, (tokens, lanes), 1)
        diagonal = lane == token + offset
        shares = []
        for block in range(rows // tokens):
            line = share_ref[block, pl.ds(me_ref[0], 1), :]
            shares.append(
                jnp.sum(
                    jnp.where(diagonal, jnp.broadcast_to(line, (tokens, lanes)), 0.0),
                    axis=-1,
                    keepdims=True,
                )
            )
        weighted = (total * jnp.concatenate(shares, axis=0)).astype(BF16)
        mine_ref[...] = weighted[: rows // 2]
        other_ref[...] = weighted[rows // 2 :]


def run_expert(me, x, shares, gate_up, down_proj, batch):
    rows, model_width = x.shape
    hidden_width = down_proj.shape[1]
    blocks, experts, lanes = shares.shape
    tokens = rows // blocks
    part = 256
    steps = hidden_width // part
    chunk = 512
    chunks = model_width // chunk
    clamp = lambda i: jnp.minimum(i, steps - 1)
    late = lambda i: jnp.maximum(i - steps, 0)
    half = jax.ShapeDtypeStruct((rows // 2, model_width), BF16)
    flops = 2 * rows * model_width * hidden_width * 3
    return pl.pallas_call(
        functools.partial(expert_kernel, steps=steps, offset=batch * tokens),
        out_shape=(half, half),
        grid_spec=pltpu.PrefetchScalarGridSpec(
            num_scalar_prefetch=1,
            grid=(steps + chunks,),
            in_specs=[
                pl.BlockSpec((rows, model_width), lambda i, me: (0, 0)),
                pl.BlockSpec((blocks, experts, lanes), lambda i, me: (0, 0, 0)),
                pl.BlockSpec((None, model_width, part), lambda i, me: (0, 0, clamp(i))),
                pl.BlockSpec((None, model_width, part), lambda i, me: (0, 0, steps + clamp(i))),
                pl.BlockSpec((None, hidden_width, chunk), lambda i, me: (0, 0, late(i))),
            ],
            out_specs=(
                pl.BlockSpec((rows // 2, chunk), lambda i, me: (0, late(i))),
                pl.BlockSpec((rows // 2, chunk), lambda i, me: (0, late(i))),
            ),
            scratch_shapes=[pltpu.VMEM((steps, rows, part), BF16)],
        ),
        compiler_params=pltpu.CompilerParams(vmem_limit_bytes=56 << 20),
        cost_estimate=pl.CostEstimate(
            flops=flops,
            bytes_accessed=2 * (3 * hidden_width * model_width + 2 * rows * model_width),
            transcendentals=rows * hidden_width,
        ),
        name="expert",
    )(me, x, shares, gate_up, gate_up, down_proj)


def ring_orders(devices):
    chips = devices // 2
    order = [2 * r if r < chips // 2 else 2 * (chips - 1 - r) + 1 for r in range(chips)]
    forward = [
        (2 * order[r] + core, 2 * order[(r + 1) % chips] + core)
        for r in range(chips)
        for core in range(2)
    ]
    backward = [(b, a) for a, b in forward]
    swap = [(i, i ^ 1) for i in range(devices)]
    return forward, backward, swap


def gather_ring(block, forward, backward, reach):
    width = block.shape[-1] // 2
    ahead = behind = block
    pairs = []
    for _ in range(reach - 1):
        ahead = lax.ppermute(ahead, "dev", forward)
        behind = lax.ppermute(behind, "dev", backward)
        pairs.append((behind, ahead))
    left = lax.ppermute(ahead[..., :width], "dev", forward)
    right = lax.ppermute(behind[..., width:], "dev", backward)
    return pairs, jnp.concatenate([left, right], axis=-1)


def add(*terms):
    total = terms[0].astype(F32)
    for term in terms[1:]:
        total = total + term.astype(F32)
    return total


def scatter_ring(near, far, forward, backward):
    far = add(*far).astype(BF16)
    width = far.shape[-1] // 2
    ahead = lax.ppermute(far[:, :width], "dev", forward)
    behind = lax.ppermute(far[:, width:], "dev", backward)
    empty = jnp.zeros_like(ahead)
    ahead = jnp.concatenate([ahead, empty], axis=-1)
    behind = jnp.concatenate([empty, behind], axis=-1)
    for up, down in reversed(near):
        ahead = lax.ppermute(add(ahead, *up).astype(BF16), "dev", forward)
        behind = lax.ppermute(add(behind, *down).astype(BF16), "dev", backward)
    return ahead, behind


def share_table(expert_ids, expert_gates, experts):
    shares = expert_gates.astype(F32)
    shares = shares / jnp.sum(shares, axis=-1, keepdims=True)
    named = lax.broadcasted_iota(jnp.int32, (experts, 1, 1, 1), 0) == expert_ids[None]
    table = jnp.sum(jnp.where(named, shares[None], 0.0), axis=-1)
    return table.reshape(experts, -1)


def to_owners(arrived, kv_heads):
    sources, positions, feat_width = arrived.shape
    grouped = arrived.reshape(sources // kv_heads, kv_heads, positions, feat_width)
    grouped = jnp.transpose(grouped, (0, 2, 1, 3))
    return grouped.reshape(sources // kv_heads * positions, kv_heads * feat_width)


def body(queries, keys_values, residual, norm_gain, gate_up, down_proj, expert_ids, expert_gates):
    devices = lax.axis_size("dev")
    batches, tokens, model_width = residual.shape
    length, feat_width = queries.shape[2:]
    kv_heads = model_width // feat_width
    experts = devices * gate_up.shape[0]
    forward, backward, swap = ring_orders(devices)
    reach = devices // 4
    split = reach // 2
    me = lax.axis_index("dev").astype(jnp.int32).reshape(1)

    table = share_table(expert_ids, expert_gates, experts)
    streams, rows_all = [], []
    for batch in range(batches):
        heads = attend(queries, keys_values, batch)
        arrived = lax.all_to_all(
            heads.reshape(devices, length // devices, feat_width),
            "dev",
            split_axis=0,
            concat_axis=0,
            tiled=True,
        )
        stream = residual[batch].astype(F32) + to_owners(arrived, kv_heads).astype(F32)
        meansq = jnp.mean(stream * stream, axis=-1, keepdims=True)
        streams.append(stream)
        rows_all.append((stream * lax.rsqrt(meansq + 1e-06) * norm_gain).astype(BF16))

    table_pairs, table_far = gather_ring(table, forward, backward, reach)
    near_tables = jnp.stack([table] + [t for pair in table_pairs[:split] for t in pair])
    far_tables = jnp.stack([t for pair in table_pairs[split:] for t in pair] + [table_far])
    near_tables = jnp.concatenate([near_tables, lax.ppermute(near_tables, "dev", swap)])
    far_tables = jnp.concatenate([far_tables, lax.ppermute(far_tables, "dev", swap)])

    pieces = []
    for batch in range(batches):
        own = rows_all[batch]
        pairs, far = gather_ring(own, forward, backward, reach)
        outs = []
        for blocks, tables in (
            ([own] + [b for pair in pairs[:split] for b in pair], near_tables),
            ([b for pair in pairs[split:] for b in pair] + [far], far_tables),
        ):
            held = jnp.concatenate(blocks, axis=0)
            swapped = lax.ppermute(held, "dev", swap)
            mine, other = run_expert(
                me, jnp.concatenate([held, swapped], axis=0), tables, gate_up, down_proj, batch
            )
            theirs = lax.ppermute(other, "dev", swap)
            for k in range(len(blocks)):
                cut = slice(k * tokens, (k + 1) * tokens)
                outs.append((mine[cut], theirs[cut]))
        near = [(outs[1 + 2 * d], outs[2 + 2 * d]) for d in range(reach - 1)]
        ahead, behind = scatter_ring(near, outs[-1], forward, backward)
        pieces.append(add(streams[batch], *outs[0], ahead, behind).astype(BF16))
    return jnp.stack(pieces, axis=0)


def solution(mesh):
    in_specs = (
        P(None, ("groups", "dev"), None, None),
        P(None, ("groups", "dev"), None, None, None),
        P(None, ("groups", "dev"), None),
        P(),
        P("dev", None, None),
        P("dev", None, None),
        P(None, ("groups", "dev"), None),
        P(None, ("groups", "dev"), None),
    )
    out_specs = P(None, ("groups", "dev"), None)
    return jax.shard_map(body, mesh=mesh, in_specs=in_specs, out_specs=out_specs, check_vma=False)
```

```python
import functools
import math

import jax
import jax.numpy as jnp
import numpy as np
from jax import lax
from jax.experimental import pallas as pl
from jax.experimental.pallas import tpu as pltpu
from jax.sharding import PartitionSpec as P

F32 = jnp.float32
BF16 = jnp.bfloat16


def attend_kernel(token_ref, q_ref, kv_ref, *refs, devices):
    out_ref, next_ref = refs[-2:]
    next_ref[...] = token_ref[...]
    length, feat_width = q_ref.shape
    context, head_size = kv_ref.shape[1:]
    scale = math.log2(math.e) / math.sqrt(head_size)
    keys, values = kv_ref[0], kv_ref[1]
    row = lax.broadcasted_iota(jnp.int32, (length, length), 0)
    col = lax.broadcasted_iota(jnp.int32, (length, length), 1)
    allowed = col <= row
    for head in range(feat_width // head_size):
        cols = slice(head * head_size, (head + 1) * head_size)
        scores = lax.dot_general(
            q_ref[:, cols], keys, (((1,), (1,)), ((), ())), preferred_element_type=F32
        )
        cached = scores[:, : context - length]
        fresh = jnp.where(allowed, scores[:, context - length :], -1e30)
        highest = jnp.maximum(
            jnp.max(cached, axis=-1, keepdims=True), jnp.max(fresh, axis=-1, keepdims=True)
        )
        grown = jnp.concatenate(
            [jnp.exp2((cached - highest) * scale), jnp.exp2((fresh - highest) * scale)], axis=1
        )
        total = jnp.sum(grown, axis=-1, keepdims=True)
        blended = jnp.dot(grown.astype(BF16), values, preferred_element_type=F32)
        out_ref[:, cols] = (blended / total).astype(BF16)
    if len(refs) == 4:
        ids_ref, gates_ref = refs[:2]
        batches, top, tokens = ids_ref.shape
        tables = []
        for batch in range(batches):
            shares = gates_ref[batch].astype(F32)
            shares = shares / jnp.sum(shares, axis=0, keepdims=True)
            expert = lax.broadcasted_iota(jnp.int32, (devices, tokens), 0)
            table = jnp.zeros((devices, tokens), F32)
            for k in range(top):
                named = expert == ids_ref[batch, k : k + 1]
                table += jnp.where(named, shares[k : k + 1], 0.0)
            tables.append(table)
        table = jnp.concatenate(tables, axis=1)
        rest = length // devices
        lines = batches * tokens
        high = table.astype(BF16).astype(F32)
        part = lax.broadcasted_iota(jnp.int32, (devices, rest, lines), 1)
        spread = [jnp.broadcast_to(x[:, None, :], part.shape) for x in (high, table - high)]
        both = jnp.where(part == 0, spread[0], jnp.where(part == 1, spread[1], 0.0))
        out_ref[:, feat_width:] = both.reshape(length, lines).astype(BF16)


def attend(token, queries, keys_values, batch, devices, *choices):
    length, feat_width = queries.shape[2:]
    context, head_size = keys_values.shape[3:]
    pairs = length * (feat_width // head_size) * context
    choices = [jnp.swapaxes(c, 1, 2) for c in choices]
    width = feat_width + (choices[0].shape[0] * choices[0].shape[2] if choices else 0)
    once = lambda shape: pl.BlockSpec(shape, lambda i: (0,) * len(shape))
    return pl.pallas_call(
        functools.partial(attend_kernel, devices=devices),
        out_shape=(
            jax.ShapeDtypeStruct((length, width), BF16),
            jax.ShapeDtypeStruct(token.shape, token.dtype),
        ),
        grid=(1,),
        in_specs=[
            once(token.shape),
            pl.BlockSpec((None, None, length, feat_width), lambda i: (batch, 0, 0, 0)),
            pl.BlockSpec((None, None, 2, context, head_size), lambda i: (batch, 0, 0, 0, 0)),
        ]
        + [once(c.shape) for c in choices],
        out_specs=(once((length, width)), once(token.shape)),
        compiler_params=pltpu.CompilerParams(vmem_limit_bytes=10 << 20),
        cost_estimate=pl.CostEstimate(
            flops=4 * pairs * head_size,
            bytes_accessed=2 * (2 * length * feat_width + 2 * context * head_size),
            transcendentals=pairs,
        ),
        name="attend",
    )(token, queries, keys_values, *choices)


def prepare_kernel(rows_ref, residual_ref, gain_ref, own_ref):
    stream = residual_ref[...].astype(F32) + rows_ref[...].astype(F32)
    meansq = jnp.mean(stream * stream, axis=-1, keepdims=True)
    own_ref[...] = (stream * lax.rsqrt(meansq + 1e-06) * gain_ref[...]).astype(BF16)


def prepare(rows, residual, norm_gain, batch):
    tokens, model_width = rows.shape
    return pl.pallas_call(
        prepare_kernel,
        out_shape=jax.ShapeDtypeStruct(rows.shape, BF16),
        grid=(1,),
        in_specs=[
            pl.BlockSpec((tokens, model_width), lambda i: (0, 0)),
            pl.BlockSpec((None, tokens, model_width), lambda i: (batch, 0, 0)),
            pl.BlockSpec((1, model_width), lambda i: (0, 0)),
        ],
        out_specs=pl.BlockSpec((tokens, model_width), lambda i: (0, 0)),
        compiler_params=pltpu.CompilerParams(vmem_limit_bytes=4 << 20),
        name="prepare",
    )(rows, residual, norm_gain.reshape(1, model_width))


def ring_place(device, step, devices):
    chips = devices // 2
    chip, core = device // 2, device % 2
    place = jnp.where(chip % 2 == 0, chip // 2, chips - 1 - chip // 2)
    place = (place + step) % chips
    chip = jnp.where(place < chips // 2, 2 * place, 2 * (chips - 1 - place) + 1)
    return 2 * chip + core


def expert_kernel(me_ref, token_ref, share_ref, gate_up_ref, down_ref, *refs, places, offset):
    blocks = len(places)
    x_refs = refs[: 2 * blocks]
    mine_ref, other_ref, next_ref, x_all, hidden_ref = refs[2 * blocks :]
    next_ref[...] = token_ref[...]
    tokens, model_width = x_refs[0].shape
    rows = blocks * tokens
    hidden_width = down_ref.shape[1]
    devices, lanes = share_ref.shape
    part = min(256, hidden_width)
    chunk = min(512, model_width)
    for block, x_ref in enumerate(x_refs):
        x_all[block * tokens : (block + 1) * tokens] = x_ref[...]
    for start in range(0, hidden_width, part):
        gate = jnp.dot(
            x_all[...], gate_up_ref[0, :, start : start + part], preferred_element_type=F32
        )
        up = jnp.dot(
            x_all[...],
            gate_up_ref[0, :, hidden_width + start : hidden_width + start + part],
            preferred_element_type=F32,
        )
        hidden_ref[:, start : start + part] = (gate / (1.0 + jnp.exp(-gate)) * up).astype(BF16)
    token = lax.broadcasted_iota(jnp.int32, (tokens, lanes), 0)
    lane = lax.broadcasted_iota(jnp.int32, (tokens, lanes), 1)
    diagonal = lane == token + offset
    shares = []
    for plane in range(2):
        for place in places:
            source = ring_place(me_ref[0], place, devices) ^ plane
            line = share_ref[pl.ds(source, 1), :]
            spread = jnp.where(diagonal, jnp.broadcast_to(line, (tokens, lanes)), 0.0)
            shares.append(jnp.sum(spread, axis=-1, keepdims=True))
    share = jnp.concatenate(shares, axis=0)
    for start in range(0, model_width, chunk):
        total = jnp.dot(
            hidden_ref[...], down_ref[0, :, start : start + chunk], preferred_element_type=F32
        )
        weighted = (total * share).astype(BF16)
        mine_ref[:, start : start + chunk] = weighted[:rows]
        other_ref[:, start : start + chunk] = weighted[rows:]


def run_expert(me, token, shares, gate_up, down_proj, held, swapped, places, batch):
    tokens, model_width = held[0].shape
    rows = len(held) * tokens
    hidden_width = down_proj.shape[1]
    whole = pl.BlockSpec(memory_space=pltpu.VMEM)
    half = jax.ShapeDtypeStruct((rows, model_width), BF16)
    gate_up = pltpu.with_memory_space_constraint(gate_up, pltpu.VMEM)
    down_proj = pltpu.with_memory_space_constraint(down_proj, pltpu.VMEM)
    return pl.pallas_call(
        functools.partial(expert_kernel, places=places, offset=batch * tokens),
        out_shape=[half, half, jax.ShapeDtypeStruct(token.shape, token.dtype)],
        in_specs=[pl.BlockSpec(memory_space=pltpu.SMEM)] + [whole] * (4 + 2 * len(held)),
        out_specs=[whole] * 3,
        scratch_shapes=[
            pltpu.VMEM((2 * rows, model_width), BF16),
            pltpu.VMEM((2 * rows, hidden_width), BF16),
        ],
        compiler_params=pltpu.CompilerParams(vmem_limit_bytes=5 << 20),
        cost_estimate=pl.CostEstimate(flops=1, bytes_accessed=1, transcendentals=0),
        name="expert",
    )(me, token, shares, gate_up, down_proj, *held, *swapped)


def load_kernel(token_ref, gate_up_ref, down_ref, next_ref, gate_up_out, down_out, sems):
    copies = [
        pltpu.make_async_copy(gate_up_ref, gate_up_out, sems.at[0]),
        pltpu.make_async_copy(down_ref, down_out, sems.at[1]),
    ]
    for copy in copies:
        copy.start()
    next_ref[...] = token_ref[...]
    for copy in copies:
        copy.wait()


def load(token, gate_up, down_proj):
    whole = pl.BlockSpec(memory_space=pltpu.VMEM)
    source = pl.BlockSpec(memory_space=pl.ANY)
    gate_up = pltpu.with_memory_space_constraint(gate_up, pltpu.HBM)
    down_proj = pltpu.with_memory_space_constraint(down_proj, pltpu.HBM)
    return pl.pallas_call(
        load_kernel,
        out_shape=[
            jax.ShapeDtypeStruct(token.shape, token.dtype),
            pltpu.VMEM(gate_up.shape, gate_up.dtype),
            pltpu.VMEM(down_proj.shape, down_proj.dtype),
        ],
        in_specs=[whole, source, source],
        out_specs=[whole, whole, whole],
        scratch_shapes=[pltpu.SemaphoreType.DMA((2,))],
        compiler_params=pltpu.CompilerParams(vmem_limit_bytes=1 << 20),
        name="load",
    )(token, gate_up, down_proj)


def ring_orders(devices):
    chips = devices // 2
    order = [2 * r if r < chips // 2 else 2 * (chips - 1 - r) + 1 for r in range(chips)]
    forward = [
        (2 * order[r] + core, 2 * order[(r + 1) % chips] + core)
        for r in range(chips)
        for core in range(2)
    ]
    backward = [(b, a) for a, b in forward]
    swap = [(i, i ^ 1) for i in range(devices)]
    return forward, backward, swap


def add(*terms):
    total = terms[0].astype(F32)
    for term in terms[1:]:
        total = total + term.astype(F32)
    return total


def to_owners(arrived, kv_heads):
    sources, positions, feat_width = arrived.shape
    grouped = arrived.reshape(sources // kv_heads, kv_heads, positions, feat_width)
    grouped = jnp.transpose(grouped, (0, 2, 1, 3))
    return grouped.reshape(sources // kv_heads * positions, kv_heads * feat_width)


class Line:
    def __init__(self):
        self.token = jnp.zeros((16, 128), F32)

    def hold(self, values):
        values, self.token = lax.optimization_barrier((values, self.token))
        return values


def body(queries, keys_values, residual, norm_gain, gate_up, down_proj, expert_ids, expert_gates):
    devices = lax.axis_size("dev")
    batches, tokens, model_width = residual.shape
    length, feat_width = queries.shape[2:]
    kv_heads = model_width // feat_width
    forward, backward, swap = ring_orders(devices)
    chips = devices // 2
    reach = chips // 2
    half = model_width // 2
    me = lax.axis_index("dev").astype(jnp.int32).reshape(1)
    send_ahead = lambda x: lax.ppermute(x, "dev", forward)
    send_behind = lambda x: lax.ppermute(x, "dev", backward)
    swapped = lambda x: lax.ppermute(x, "dev", swap)
    line = Line()

    queries = pltpu.with_memory_space_constraint(queries, pltpu.HBM)
    keys_values = pltpu.with_memory_space_constraint(keys_values, pltpu.HBM)

    def exchange(heads):
        return lax.all_to_all(
            heads.reshape(devices, length // devices, -1),
            "dev",
            split_axis=0,
            concat_axis=0,
            tiled=True,
        )

    class Chain:
        def __init__(self, batch):
            self.batch = batch
            self.held = {}
            self.others = {}
            self.outs = {}
            self.pending = []

        def prepare(self, arrived):
            arrived = line.hold(arrived)
            self.rows = to_owners(arrived[..., :feat_width], kv_heads)
            own = prepare(self.rows, residual, norm_gain, self.batch)
            self.held[0] = [own]
            self.moving = [own, own]
            return arrived

        def start(self, step):
            if step > reach:
                self.start_back(step - reach)
            elif step < reach:
                self.moving = [send_ahead(self.moving[0]), send_behind(self.moving[1])]
            else:
                self.moving = [
                    send_ahead(self.moving[0][:, :half]),
                    send_behind(self.moving[1][:, half:]),
                ]

        def land(self, step):
            self.moving = line.hold(self.moving)
            if step < reach:
                self.held[step] = [self.moving[1], self.moving[0]]
            elif step == reach:
                self.held[step] = [jnp.concatenate(self.moving, axis=1)]

        def swap(self, step):
            self.others[step] = [swapped(x) for x in self.held[step]]

        def expert(self, step):
            places = [step] if step in (0, reach) else [step, chips - step]
            mine, other, line.token = run_expert(
                me, line.token, shares, gate_up, down_proj, self.held[step], self.others[step],
                places, self.batch,
            )
            self.outs[step] = [mine, swapped(other)]

        def settle(self, step):
            self.outs[step] = line.hold(self.outs[step])

        def start_back(self, step):
            mine, other = self.outs[reach + 1 - step]
            if step == 1:
                total = add(mine, other).astype(BF16)
                sums = [total[:, :half], total[:, half:]]
            else:
                ahead, behind = self.moving
                if step == 2:
                    empty = jnp.zeros_like(ahead)
                    ahead = jnp.concatenate([ahead, empty], axis=1)
                    behind = jnp.concatenate([empty, behind], axis=1)
                sums = [
                    add(ahead, mine[:tokens], other[:tokens]).astype(BF16),
                    add(behind, mine[tokens:], other[tokens:]).astype(BF16),
                ]
            sums = line.hold(sums)
            self.moving = [send_ahead(sums[0]), send_behind(sums[1])]

        def finish(self):
            return add(
                residual[self.batch], self.rows, *self.outs[0], *self.moving
            ).astype(BF16)

    heads, line.token = attend(
        line.token, queries, keys_values, 0, devices, expert_ids, expert_gates
    )
    arrived = exchange(heads)
    later, line.token = attend(line.token, queries, keys_values, 1, devices)
    line.token, gate_up, down_proj = load(line.token, gate_up, down_proj)

    a, b = [Chain(batch) for batch in range(batches)]
    arrived = a.prepare(arrived)
    shares = arrived[:, 0, feat_width:].astype(F32) + arrived[:, 1, feat_width:].astype(F32)
    later, a.held[0][0] = lax.optimization_barrier((later, a.held[0][0]))
    a.moving = a.held[0] * 2
    arrived = exchange(later)
    a.start(1)
    a.swap(0)
    a.expert(0)
    a.land(1)
    a.swap(1)
    a.start(2)
    a.land(2)
    a.swap(2)
    a.start(3)
    b.prepare(arrived)
    b.start(1)
    b.swap(0)
    a.settle(0)
    for step in range(3, reach + 1):
        a.expert(step - 2)
        a.land(step)
        a.swap(step)
        if step < reach:
            a.start(step + 1)
        b.land(step - 2)
        b.swap(step - 2)
        b.start(step - 1)
        if step > 3:
            a.settle(step - 3)
    a.expert(reach - 1)
    a.expert(reach)
    b.land(reach - 1)
    b.swap(reach - 1)
    b.start(reach)
    a.settle(reach - 2)
    b.expert(0)
    a.settle(reach - 1)
    a.settle(reach)
    a.start(reach + 1)
    b.land(reach)
    b.swap(reach)
    b.expert(1)
    a.land(reach + 1)
    a.start(reach + 2)
    for step in range(2, reach):
        b.expert(step)
        b.settle(step - 2)
    b.expert(reach)
    a.land(reach + 2)
    a.start(reach + 3)
    b.settle(reach - 2)
    b.settle(reach - 1)
    b.settle(reach)
    b.start(reach + 1)
    for step in range(reach + 3, 2 * reach):
        a.land(step)
        a.start(step + 1)
        b.land(step - 2)
        b.start(step - 1)
    a.land(2 * reach)
    for step in range(2 * reach - 2, 2 * reach):
        b.land(step)
        b.start(step + 1)
    b.land(2 * reach)
    return jnp.stack([a.finish(), b.finish()], axis=0)


def solution(mesh):
    in_specs = (
        P(None, ("groups", "dev"), None, None),
        P(None, ("groups", "dev"), None, None, None),
        P(None, ("groups", "dev"), None),
        P(),
        P("dev", None, None),
        P("dev", None, None),
        P(None, ("groups", "dev"), None),
        P(None, ("groups", "dev"), None),
    )
    out_specs = P(None, ("groups", "dev"), None)
    return jax.shard_map(body, mesh=mesh, in_specs=in_specs, out_specs=out_specs, check_vma=False)
```

```python
import functools
import math

import jax
import jax.numpy as jnp
import numpy as np
from jax import lax
from jax.experimental import pallas as pl
from jax.experimental.pallas import tpu as pltpu
from jax.sharding import PartitionSpec as P

F32 = jnp.float32
BF16 = jnp.bfloat16


def attend_kernel(q_ref, kv_ref, ids_ref, gates_ref, out_ref, *, devices):
    length, feat_width = q_ref.shape
    context, head_size = kv_ref.shape[1:]
    positions = length // devices
    scale = math.log2(math.e) / math.sqrt(head_size)
    keys, values = kv_ref[0], kv_ref[1]
    row = lax.broadcasted_iota(jnp.int32, (length, length), 0)
    col = lax.broadcasted_iota(jnp.int32, (length, length), 1)
    allowed = col <= row

    def put(cols, value):
        if len(out_ref.shape) == 3:
            value = value.reshape(devices, positions, value.shape[-1])
            out_ref[:, :, cols] = value.astype(BF16)
        else:
            out_ref[:, cols] = value.astype(BF16)

    for head in range(feat_width // head_size):
        cols = slice(head * head_size, (head + 1) * head_size)
        scores = lax.dot_general(
            q_ref[:, cols], keys, (((1,), (1,)), ((), ())), preferred_element_type=F32
        )
        cached = scores[:, : context - length]
        fresh = jnp.where(allowed, scores[:, context - length :], -1e30)
        highest = jnp.maximum(
            jnp.max(cached, axis=-1, keepdims=True), jnp.max(fresh, axis=-1, keepdims=True)
        )
        grown = jnp.concatenate(
            [jnp.exp2((cached - highest) * scale), jnp.exp2((fresh - highest) * scale)], axis=1
        )
        total = jnp.sum(grown, axis=-1, keepdims=True)
        blended = jnp.dot(grown.astype(BF16), values, preferred_element_type=F32)
        put(cols, blended / total)

    batches, top, tokens = ids_ref.shape
    lines = batches * tokens
    last = slice(feat_width, feat_width + lines)
    tables = []
    for batch in range(batches):
        shares = gates_ref[batch].astype(F32)
        shares = shares / jnp.sum(shares, axis=0, keepdims=True)
        expert = lax.broadcasted_iota(jnp.int32, (devices, tokens), 0)
        table = jnp.zeros((devices, tokens), F32)
        for k in range(top):
            named = expert == ids_ref[batch, k : k + 1]
            table += jnp.where(named, shares[k : k + 1], 0.0)
        tables.append(table)
    table = jnp.concatenate(tables, axis=1)
    high = table.astype(BF16).astype(F32)
    part = lax.broadcasted_iota(jnp.int32, (devices, positions, lines), 1)
    spread = [jnp.broadcast_to(x[:, None, :], part.shape) for x in (high, table - high)]
    both = jnp.where(part == 0, spread[0], jnp.where(part == 1, spread[1], 0.0))
    put(last, both.reshape(length, lines))


def attend(queries, keys_values, expert_ids, expert_gates, devices):
    batches, _, length, feat_width = queries.shape
    context, head_size = keys_values.shape[3:]
    positions = length // devices
    pairs = batches * length * (feat_width // head_size) * context
    queries, keys_values, *choices = [
        pltpu.with_memory_space_constraint(x, pltpu.HBM)
        for x in (
            queries,
            keys_values,
            jnp.swapaxes(expert_ids, 1, 2),
            jnp.swapaxes(expert_gates, 1, 2),
        )
    ]
    width = feat_width + batches * expert_ids.shape[1]
    direct = positions % 8 == 0
    if direct:
        shape = (devices, batches, positions, width)
        out_spec = pl.BlockSpec((devices, None, positions, width), lambda i: (0, i, 0, 0))
    else:
        shape = (batches, length, width)
        out_spec = pl.BlockSpec((None, length, width), lambda i: (i, 0, 0))
    rows = pl.pallas_call(
        functools.partial(attend_kernel, devices=devices),
        out_shape=jax.ShapeDtypeStruct(shape, BF16),
        grid=(batches,),
        in_specs=[
            pl.BlockSpec((None, None, length, feat_width), lambda i: (i, 0, 0, 0)),
            pl.BlockSpec((None, None, 2, context, head_size), lambda i: (i, 0, 0, 0, 0)),
        ]
        + [pl.BlockSpec(c.shape, lambda i: (0, 0, 0)) for c in choices],
        out_specs=out_spec,
        compiler_params=pltpu.CompilerParams(vmem_limit_bytes=24 << 20),
        cost_estimate=pl.CostEstimate(
            flops=4 * pairs * head_size,
            bytes_accessed=2 * batches * (2 * length * feat_width + 2 * context * head_size),
            transcendentals=pairs,
        ),
        name="attend",
    )(queries, keys_values, *choices)
    if not direct:
        rows = jnp.swapaxes(rows.reshape(batches, devices, positions, width), 0, 1)
    return rows


def prepare_kernel(arrived_ref, residual_ref, gain_ref, left_ref, right_ref, *stream_refs, kv_heads):
    batches, tokens, model_width = residual_ref.shape
    feat_width = model_width // kv_heads
    half = model_width // batches
    for batch, stream_ref in enumerate(stream_refs):
        if len(arrived_ref.shape) == 4:
            sources, _, positions, _ = arrived_ref.shape
            for source in range(sources):
                first = source // kv_heads * positions
                left = source % kv_heads * feat_width
                stream_ref[first : first + positions, left : left + feat_width] = arrived_ref[
                    source, batch, :, :feat_width
                ].astype(F32)
            rows = stream_ref[...]
        else:
            rows = arrived_ref[batch].astype(F32)
        stream = residual_ref[batch].astype(F32) + rows
        stream_ref[...] = stream
        meansq = jnp.mean(stream * stream, axis=-1, keepdims=True)
        own = (stream * lax.rsqrt(meansq + 1e-06) * gain_ref[...]).astype(BF16)
        left_ref[:, batch * half : (batch + 1) * half] = own[:, :half]
        right_ref[:, batch * half : (batch + 1) * half] = own[:, half:]


def prepare(arrived, residual, norm_gain, kv_heads):
    batches, tokens, model_width = residual.shape
    sources, _, positions, _ = arrived.shape
    feat_width = model_width // kv_heads
    if positions % 8:
        rows = arrived[..., :feat_width]
        rows = rows.reshape(sources // kv_heads, kv_heads, batches, positions, feat_width)
        arrived = jnp.transpose(rows, (2, 0, 3, 1, 4)).reshape(batches, tokens, model_width)
    row = (tokens, model_width)
    whole = pl.BlockSpec(memory_space=pltpu.VMEM)
    left, right, *streams = pl.pallas_call(
        functools.partial(prepare_kernel, kv_heads=kv_heads),
        out_shape=[jax.ShapeDtypeStruct(row, BF16)] * 2
        + [jax.ShapeDtypeStruct(row, F32)] * batches,
        in_specs=[whole] * 3,
        out_specs=[whole] * (2 + batches),
        compiler_params=pltpu.CompilerParams(vmem_limit_bytes=8 << 20),
        name="prepare",
    )(arrived, residual, norm_gain.reshape(1, model_width))
    return left, right, streams


def ring_place(device, step, devices):
    chips = devices // 2
    chip, core = device // 2, device % 2
    place = jnp.where(chip % 2 == 0, chip // 2, chips - 1 - chip // 2)
    place = (place + step) % chips
    chip = jnp.where(place < chips // 2, 2 * place, 2 * (chips - 1 - place) + 1)
    return 2 * chip + core


def expert_kernel(me_ref, token_ref, share_a, share_b, gate_up_a, gate_up_b, down_a, down_b, *refs, places):
    *held_refs, out_ref, next_ref, x_all, hidden_a, hidden_b = refs
    next_ref[...] = token_ref[...]
    tokens, model_width = held_refs[0].shape
    half = model_width // 2
    blocks = len(places)
    hidden_width = down_a.shape[1]
    devices, lanes = share_a.shape
    part = min(256, hidden_width)
    chunk = min(512, half)

    row_of = lambda block, batch: (block * 2 + batch) * tokens
    for block in range(blocks):
        for side in range(2):
            cols = slice(side * half, (side + 1) * half)
            for batch in range(2):
                row = row_of(block, batch)
                came = slice(batch * half, (batch + 1) * half)
                x_all[row : row + tokens, cols] = held_refs[2 * block + side][:, came]
    token = lax.broadcasted_iota(jnp.int32, (tokens, lanes), 0)
    lane = lax.broadcasted_iota(jnp.int32, (tokens, lanes), 1)
    for share_ref, gate_up_ref, hidden_ref in (
        (share_a, gate_up_a, hidden_a),
        (share_b, gate_up_b, hidden_b),
    ):
        shares = []
        for place in places:
            source = ring_place(me_ref[0], place, devices)
            line = jnp.broadcast_to(share_ref[pl.ds(source, 1), :], (tokens, lanes))
            for batch in range(2):
                spread = jnp.where(lane == token + batch * tokens, line, 0.0)
                shares.append(jnp.sum(spread, axis=-1, keepdims=True))
        share = jnp.concatenate(shares, axis=0)
        for start in range(0, hidden_width, part):
            gate = jnp.dot(
                x_all[...], gate_up_ref[0, :, start : start + part], preferred_element_type=F32
            )
            up = jnp.dot(
                x_all[...],
                gate_up_ref[0, :, hidden_width + start : hidden_width + start + part],
                preferred_element_type=F32,
            )
            act = gate / (1.0 + jnp.exp(-gate)) * up
            hidden_ref[:, start : start + part] = (act * share).astype(BF16)
    for start in range(0, model_width, chunk):
        cols = slice(start, start + chunk)
        total = jnp.dot(hidden_a[...], down_a[0, :, cols], preferred_element_type=F32)
        total += jnp.dot(hidden_b[...], down_b[0, :, cols], preferred_element_type=F32)
        weighted = total.astype(BF16)
        side, left = start // half, start % half
        for block in range(blocks):
            rows = slice((2 * block + side) * tokens, (2 * block + side + 1) * tokens)
            for batch in range(2):
                row = row_of(block, batch)
                goes = slice(batch * half + left, batch * half + left + chunk)
                out_ref[rows, goes] = weighted[row : row + tokens]


def run_experts(me, token, shares, weights, held, places):
    tokens, model_width = held[0].shape
    rows = tokens * len(held)
    hidden_width = weights[2].shape[1]
    whole = pl.BlockSpec(memory_space=pltpu.VMEM)
    return pl.pallas_call(
        functools.partial(expert_kernel, places=places),
        out_shape=[
            jax.ShapeDtypeStruct((rows, model_width), BF16),
            jax.ShapeDtypeStruct(token.shape, token.dtype),
        ],
        in_specs=[pl.BlockSpec(memory_space=pltpu.SMEM)] + [whole] * (7 + len(held)),
        out_specs=[whole] * 2,
        scratch_shapes=[
            pltpu.VMEM((rows, model_width), BF16),
            pltpu.VMEM((rows, hidden_width), BF16),
            pltpu.VMEM((rows, hidden_width), BF16),
        ],
        compiler_params=pltpu.CompilerParams(vmem_limit_bytes=10 << 20),
        cost_estimate=pl.CostEstimate(flops=1, bytes_accessed=1, transcendentals=0),
        name="experts",
    )(me, token, *shares, *weights, *held)


def load_kernel(token_ref, *refs):
    count = len(refs) // 2 - 1
    next_ref, *out_refs = refs[count:-1]
    copies = [
        pltpu.make_async_copy(ref, out_ref, refs[-1].at[k])
        for k, (ref, out_ref) in enumerate(zip(refs[:count], out_refs))
    ]
    for copy in copies:
        copy.start()
    next_ref[...] = token_ref[...]
    for copy in copies:
        copy.wait()


def load(token, *arrays):
    whole = pl.BlockSpec(memory_space=pltpu.VMEM)
    place = pl.BlockSpec(memory_space=pl.ANY)
    return pl.pallas_call(
        load_kernel,
        out_shape=[jax.ShapeDtypeStruct(x.shape, x.dtype) for x in (token, *arrays)],
        in_specs=[whole] + [place] * len(arrays),
        out_specs=[whole] * (1 + len(arrays)),
        scratch_shapes=[pltpu.SemaphoreType.DMA((len(arrays),))],
        compiler_params=pltpu.CompilerParams(vmem_limit_bytes=1 << 20),
        cost_estimate=pl.CostEstimate(flops=1, bytes_accessed=1, transcendentals=0),
        name="load",
    )(token, *arrays)


def ring_orders(devices):
    chips = devices // 2
    order = [2 * r if r < chips // 2 else 2 * (chips - 1 - r) + 1 for r in range(chips)]
    forward = [
        (2 * order[r] + core, 2 * order[(r + 1) % chips] + core)
        for r in range(chips)
        for core in range(2)
    ]
    backward = [(b, a) for a, b in forward]
    swap = [(i, i ^ 1) for i in range(devices)]
    return forward, backward, swap


def fence_kernel(token_ref, *refs):
    refs[len(refs) // 2][...] = token_ref[...]


def fence(token, values):
    place = pl.BlockSpec(memory_space=pl.ANY)
    whole = pl.BlockSpec(memory_space=pltpu.VMEM)
    token, *values = pl.pallas_call(
        fence_kernel,
        out_shape=[jax.ShapeDtypeStruct(x.shape, x.dtype) for x in (token, *values)],
        in_specs=[whole] + [place] * len(values),
        out_specs=[whole] + [place] * len(values),
        input_output_aliases={k: k for k in range(1, len(values) + 1)},
        compiler_params=pltpu.CompilerParams(vmem_limit_bytes=1 << 20),
        cost_estimate=pl.CostEstimate(flops=1, bytes_accessed=4 << 20, transcendentals=0),
        name="fence",
    )(token, *values)
    return token, values


def merge_kernel(token_ref, terms_ref, *refs, cuts):
    *moving, next_ref, ahead_ref, behind_ref = refs
    next_ref[...] = token_ref[...]
    for way, out_ref in enumerate((ahead_ref, behind_ref)):
        total = terms_ref[cuts[way]]
        if moving:
            total = (total.astype(F32) + moving[way][...].astype(F32)).astype(BF16)
        out_ref[...] = total


def merge(token, terms, moving, cuts):
    whole = pl.BlockSpec(memory_space=pltpu.VMEM)
    part = jax.ShapeDtypeStruct((cuts[0].stop - cuts[0].start, terms.shape[1]), BF16)
    return pl.pallas_call(
        functools.partial(merge_kernel, cuts=cuts),
        out_shape=[jax.ShapeDtypeStruct(token.shape, token.dtype), part, part],
        in_specs=[whole] * (2 + len(moving)),
        out_specs=[whole] * 3,
        compiler_params=pltpu.CompilerParams(vmem_limit_bytes=4 << 20),
        cost_estimate=pl.CostEstimate(flops=1, bytes_accessed=1, transcendentals=0),
        name="merge",
    )(token, terms, *moving)


def finish_kernel(terms_ref, *refs):
    *sum_refs, out_ref = refs
    batches, tokens, model_width = out_ref.shape
    stream_refs, sum_refs = sum_refs[:batches], sum_refs[batches:]
    half = model_width // batches
    for side in range(2):
        total = terms_ref[side * tokens : (side + 1) * tokens].astype(F32)
        for sum_ref in sum_refs[2 * side : 2 * side + 2]:
            total = total + sum_ref[...].astype(F32)
        cols = slice(side * half, (side + 1) * half)
        for batch, stream_ref in enumerate(stream_refs):
            came = total[:, batch * half : (batch + 1) * half]
            out_ref[batch, :, cols] = (stream_ref[:, cols] + came).astype(BF16)


def finish(terms, streams, sums):
    whole = pl.BlockSpec(memory_space=pltpu.VMEM)
    return pl.pallas_call(
        finish_kernel,
        out_shape=jax.ShapeDtypeStruct((len(streams), *streams[0].shape), BF16),
        in_specs=[whole] * (1 + len(streams) + len(sums)),
        out_specs=whole,
        compiler_params=pltpu.CompilerParams(vmem_limit_bytes=8 << 20),
        name="finish",
    )(terms, *streams, *sums)


class Line:
    def __init__(self):
        self.token = jnp.zeros((16, 128), F32)

    def hold(self, values):
        self.token, values = fence(self.token, values)
        return values


def body(queries, keys_values, residual, norm_gain, gate_up, down_proj, expert_ids, expert_gates):
    devices = lax.axis_size("dev")
    batches, tokens, model_width = residual.shape
    length, feat_width = queries.shape[2:]
    kv_heads = model_width // feat_width
    forward, backward, swap = ring_orders(devices)
    chips = devices // 2
    reach = chips // 2
    half = model_width // 2
    me = lax.axis_index("dev").astype(jnp.int32).reshape(1)
    me, queries = lax.optimization_barrier((me, queries))
    send_ahead = lambda x: lax.ppermute(x, "dev", forward)
    send_behind = lambda x: lax.ppermute(x, "dev", backward)
    swapped = lambda x: lax.ppermute(x, "dev", swap)
    line = Line()

    gate_up_b, down_b = swapped(gate_up), swapped(down_proj)
    rows = attend(queries, keys_values, expert_ids, expert_gates, devices)
    arrived = lax.all_to_all(
        rows.reshape(devices, -1, rows.shape[-1]), "dev", split_axis=0, concat_axis=0, tiled=True
    )
    arrived, gate_up_b, down_b = line.hold([arrived, gate_up_b, down_b])
    arrived = arrived.reshape(rows.shape)
    left, right, streams = prepare(arrived, residual, norm_gain, kv_heads)
    shares = arrived[:, 0, 0, feat_width:].astype(F32) + arrived[:, 0, 1, feat_width:].astype(F32)
    shares = [shares, swapped(shares)]

    class Chain:
        def __init__(self, ahead, behind):
            self.moving = [ahead, behind]

        def send(self):
            self.moving = [send_ahead(self.moving[0]), send_behind(self.moving[1])]

        def land(self):
            self.moving = line.hold(self.moving)

    long, short = Chain(left, right), Chain(right, left)
    held = {0: [left, right]}
    terms = {}

    def experts(step):
        places = [step] if step in (0, reach) else [step, chips - step]
        terms[step], line.token = run_experts(
            me, line.token, shares, weights, held[step], places
        )

    def send_back(chain, step, first=False):
        sides = (0, 1) if step == reach else (0, 3) if chain is long else (1, 2)
        cuts = [slice(side * tokens, (side + 1) * tokens) for side in sides]
        line.token, *chain.moving = merge(
            line.token, terms[step], [] if first else chain.moving, cuts
        )
        chain.send()

    short.send()
    long.send()
    line.token, gate_up_b = load(line.token, gate_up_b)
    weights = [gate_up, gate_up_b, down_proj, down_b]
    for step in range(1, reach):
        short.land()
        came_right, came_left = short.moving
        if step < reach - 1:
            short.send()
        long.land()
        held[step] = [came_left, long.moving[1], long.moving[0], came_right]
        long.send()
        if step < reach - 1:
            experts(step - 1)
    experts(reach - 1)
    send_back(short, reach - 1, True)
    long.land()
    held[reach] = long.moving
    experts(reach)
    send_back(long, reach, True)
    experts(reach - 2)
    for step in range(reach - 2, 0, -1):
        send_back(short, step)
        send_back(long, step + 1)
    short.land()
    send_back(long, 1)
    ahead, behind = long.moving
    short_ahead, short_behind = short.moving
    return finish(terms[0], streams, [ahead, short_behind, behind, short_ahead])


def solution(mesh):
    in_specs = (
        P(None, ("groups", "dev"), None, None),
        P(None, ("groups", "dev"), None, None, None),
        P(None, ("groups", "dev"), None),
        P(),
        P("dev", None, None),
        P("dev", None, None),
        P(None, ("groups", "dev"), None),
        P(None, ("groups", "dev"), None),
    )
    out_specs = P(None, ("groups", "dev"), None)
    return jax.shard_map(body, mesh=mesh, in_specs=in_specs, out_specs=out_specs, check_vma=False)
```

```python
import functools
import math

import jax
import jax.numpy as jnp
import numpy as np
from jax import lax
from jax.experimental import pallas as pl
from jax.experimental.pallas import tpu as pltpu
from jax.sharding import PartitionSpec as P

F32 = jnp.float32
BF16 = jnp.bfloat16


def attend_kernel(q_ref, kv_ref, ids_ref, gates_ref, out_ref, values_ref, *, devices):
    length, feat_width = q_ref.shape
    context, head_size = kv_ref.shape[1:]
    positions = length // devices
    scale = math.log2(math.e) / math.sqrt(head_size)
    keys = kv_ref[0]
    values_ref[:, :head_size] = kv_ref[1]
    values_ref[:, head_size:] = jnp.ones((context, head_size), BF16)
    row = lax.broadcasted_iota(jnp.int32, (length, length), 0)
    col = lax.broadcasted_iota(jnp.int32, (length, length), 1)
    heads = feat_width // head_size
    stack = 2 if heads % 2 == 0 else 1
    allowed = jnp.concatenate([col <= row] * stack, axis=0)

    def put(cols, value):
        if len(out_ref.shape) == 3:
            value = value.reshape(devices, positions, value.shape[-1])
            out_ref[:, :, cols] = value.astype(BF16)
        else:
            out_ref[:, cols] = value.astype(BF16)

    for first in range(0, heads, stack):
        cols = [slice(h * head_size, (h + 1) * head_size) for h in range(first, first + stack)]
        scores = lax.dot_general(
            jnp.concatenate([q_ref[:, c] for c in cols], axis=0),
            keys,
            (((1,), (1,)), ((), ())),
            preferred_element_type=F32,
        )
        cached = scores[:, : context - length]
        fresh = jnp.where(allowed, scores[:, context - length :], -1e30)
        highest = jnp.maximum(
            jnp.max(cached, axis=-1, keepdims=True), jnp.max(fresh, axis=-1, keepdims=True)
        )
        grown = jnp.concatenate(
            [jnp.exp2((cached - highest) * scale), jnp.exp2((fresh - highest) * scale)], axis=1
        )
        both = jnp.dot(grown.astype(BF16), values_ref[...], preferred_element_type=F32)
        blended = both[:, :head_size] / both[:, head_size:]
        for k, c in enumerate(cols):
            put(c, blended[k * length : (k + 1) * length])

    batches, top, tokens = ids_ref.shape
    lines = batches * tokens
    last = slice(feat_width, feat_width + lines)
    tables = []
    for batch in range(batches):
        shares = gates_ref[batch].astype(F32)
        shares = shares / jnp.sum(shares, axis=0, keepdims=True)
        expert = lax.broadcasted_iota(jnp.int32, (devices, tokens), 0)
        table = jnp.zeros((devices, tokens), F32)
        for k in range(top):
            named = expert == ids_ref[batch, k : k + 1]
            table += jnp.where(named, shares[k : k + 1], 0.0)
        tables.append(table)
    table = jnp.concatenate(tables, axis=1)
    high = table.astype(BF16).astype(F32)
    part = lax.broadcasted_iota(jnp.int32, (devices, positions, lines), 1)
    spread = [jnp.broadcast_to(x[:, None, :], part.shape) for x in (high, table - high)]
    both = jnp.where(part == 0, spread[0], jnp.where(part == 1, spread[1], 0.0))
    put(last, both.reshape(length, lines))


def attend(queries, keys_values, expert_ids, expert_gates, devices):
    batches, _, length, feat_width = queries.shape
    context, head_size = keys_values.shape[3:]
    positions = length // devices
    pairs = batches * length * (feat_width // head_size) * context
    queries, keys_values, *choices = [
        pltpu.with_memory_space_constraint(x, pltpu.HBM)
        for x in (
            queries,
            keys_values,
            jnp.swapaxes(expert_ids, 1, 2),
            jnp.swapaxes(expert_gates, 1, 2),
        )
    ]
    width = feat_width + batches * expert_ids.shape[1]
    direct = positions % 8 == 0
    if direct:
        shape = (devices, batches, positions, width)
        out_spec = pl.BlockSpec((devices, None, positions, width), lambda i: (0, i, 0, 0))
    else:
        shape = (batches, length, width)
        out_spec = pl.BlockSpec((None, length, width), lambda i: (i, 0, 0))
    rows = pl.pallas_call(
        functools.partial(attend_kernel, devices=devices),
        out_shape=jax.ShapeDtypeStruct(shape, BF16),
        grid=(batches,),
        in_specs=[
            pl.BlockSpec((None, None, length, feat_width), lambda i: (i, 0, 0, 0)),
            pl.BlockSpec((None, None, 2, context, head_size), lambda i: (i, 0, 0, 0, 0)),
        ]
        + [pl.BlockSpec(c.shape, lambda i: (0, 0, 0)) for c in choices],
        out_specs=out_spec,
        scratch_shapes=[pltpu.VMEM((context, 2 * head_size), BF16)],
        compiler_params=pltpu.CompilerParams(vmem_limit_bytes=24 << 20),
        cost_estimate=pl.CostEstimate(
            flops=4 * pairs * head_size,
            bytes_accessed=2 * batches * (2 * length * feat_width + 2 * context * head_size),
            transcendentals=pairs,
        ),
        name="attend",
    )(queries, keys_values, *choices)
    if not direct:
        rows = jnp.swapaxes(rows.reshape(batches, devices, positions, width), 0, 1)
    return rows


def prepare_kernel(arrived_ref, residual_ref, gain_ref, left_ref, right_ref, *stream_refs, kv_heads):
    batches, tokens, model_width = residual_ref.shape
    feat_width = model_width // kv_heads
    half = model_width // batches
    for batch, stream_ref in enumerate(stream_refs):
        if len(arrived_ref.shape) == 4:
            sources, _, positions, _ = arrived_ref.shape
            for source in range(sources):
                first = source // kv_heads * positions
                left = source % kv_heads * feat_width
                stream_ref[first : first + positions, left : left + feat_width] = arrived_ref[
                    source, batch, :, :feat_width
                ].astype(F32)
            rows = stream_ref[...]
        else:
            rows = arrived_ref[batch].astype(F32)
        stream = residual_ref[batch].astype(F32) + rows
        stream_ref[...] = stream
        meansq = jnp.mean(stream * stream, axis=-1, keepdims=True)
        own = (stream * lax.rsqrt(meansq + 1e-06) * gain_ref[...]).astype(BF16)
        left_ref[:, batch * half : (batch + 1) * half] = own[:, :half]
        right_ref[:, batch * half : (batch + 1) * half] = own[:, half:]


def prepare(arrived, residual, norm_gain, kv_heads):
    batches, tokens, model_width = residual.shape
    sources, _, positions, _ = arrived.shape
    feat_width = model_width // kv_heads
    if positions % 8:
        rows = arrived[..., :feat_width]
        rows = rows.reshape(sources // kv_heads, kv_heads, batches, positions, feat_width)
        arrived = jnp.transpose(rows, (2, 0, 3, 1, 4)).reshape(batches, tokens, model_width)
    row = (tokens, model_width)
    whole = pl.BlockSpec(memory_space=pltpu.VMEM)
    left, right, *streams = pl.pallas_call(
        functools.partial(prepare_kernel, kv_heads=kv_heads),
        out_shape=[jax.ShapeDtypeStruct(row, BF16)] * 2
        + [jax.ShapeDtypeStruct(row, F32)] * batches,
        in_specs=[whole] * 3,
        out_specs=[whole] * (2 + batches),
        compiler_params=pltpu.CompilerParams(vmem_limit_bytes=8 << 20),
        name="prepare",
    )(arrived, residual, norm_gain.reshape(1, model_width))
    return left, right, streams


def ring_place(device, step, devices):
    chips = devices // 2
    chip, core = device // 2, device % 2
    place = jnp.where(chip % 2 == 0, chip // 2, chips - 1 - chip // 2)
    place = (place + step) % chips
    chip = jnp.where(place < chips // 2, 2 * place, 2 * (chips - 1 - place) + 1)
    return 2 * chip + core


def expert_kernel(me_ref, token_ref, share_a, share_b, gate_up_a, gate_up_b, down_a, down_b, *refs, places):
    *held_refs, out_ref, next_ref, x_all, hidden_a, hidden_b = refs
    next_ref[...] = token_ref[...]
    tokens, model_width = held_refs[0].shape
    half = model_width // 2
    blocks = len(places)
    hidden_width = down_a.shape[1]
    devices, lanes = share_a.shape
    part = min(256, hidden_width)
    chunk = min(512, half)

    row_of = lambda block, batch: (block * 2 + batch) * tokens
    for block in range(blocks):
        for side in range(2):
            cols = slice(side * half, (side + 1) * half)
            for batch in range(2):
                row = row_of(block, batch)
                came = slice(batch * half, (batch + 1) * half)
                x_all[row : row + tokens, cols] = held_refs[2 * block + side][:, came]
    token = lax.broadcasted_iota(jnp.int32, (tokens, lanes), 0)
    lane = lax.broadcasted_iota(jnp.int32, (tokens, lanes), 1)
    for share_ref, gate_up_ref, hidden_ref in (
        (share_a, gate_up_a, hidden_a),
        (share_b, gate_up_b, hidden_b),
    ):
        shares = []
        for place in places:
            source = ring_place(me_ref[0], place, devices)
            line = jnp.broadcast_to(share_ref[pl.ds(source, 1), :], (tokens, lanes))
            for batch in range(2):
                spread = jnp.where(lane == token + batch * tokens, line, 0.0)
                shares.append(jnp.sum(spread, axis=-1, keepdims=True))
        share = jnp.concatenate(shares, axis=0)
        for start in range(0, hidden_width, part):
            gate = jnp.dot(
                x_all[...], gate_up_ref[0, :, start : start + part], preferred_element_type=F32
            )
            up = jnp.dot(
                x_all[...],
                gate_up_ref[0, :, hidden_width + start : hidden_width + start + part],
                preferred_element_type=F32,
            )
            act = gate / (1.0 + jnp.exp(-gate)) * up
            hidden_ref[:, start : start + part] = (act * share).astype(BF16)
    for start in range(0, model_width, chunk):
        cols = slice(start, start + chunk)
        total = jnp.dot(hidden_a[...], down_a[0, :, cols], preferred_element_type=F32)
        total += jnp.dot(hidden_b[...], down_b[0, :, cols], preferred_element_type=F32)
        weighted = total.astype(BF16)
        side, left = start // half, start % half
        for block in range(blocks):
            rows = slice((2 * block + side) * tokens, (2 * block + side + 1) * tokens)
            for batch in range(2):
                row = row_of(block, batch)
                goes = slice(batch * half + left, batch * half + left + chunk)
                out_ref[rows, goes] = weighted[row : row + tokens]


def run_experts(me, token, shares, weights, held, places):
    tokens, model_width = held[0].shape
    rows = tokens * len(held)
    hidden_width = weights[2].shape[1]
    whole = pl.BlockSpec(memory_space=pltpu.VMEM)
    return pl.pallas_call(
        functools.partial(expert_kernel, places=places),
        out_shape=[
            jax.ShapeDtypeStruct((rows, model_width), BF16),
            jax.ShapeDtypeStruct(token.shape, token.dtype),
        ],
        in_specs=[pl.BlockSpec(memory_space=pltpu.SMEM)] + [whole] * (7 + len(held)),
        out_specs=[whole] * 2,
        scratch_shapes=[
            pltpu.VMEM((rows, model_width), BF16),
            pltpu.VMEM((rows, hidden_width), BF16),
            pltpu.VMEM((rows, hidden_width), BF16),
        ],
        compiler_params=pltpu.CompilerParams(vmem_limit_bytes=10 << 20),
        cost_estimate=pl.CostEstimate(flops=1, bytes_accessed=1, transcendentals=0),
        name="experts",
    )(me, token, *shares, *weights, *held)


def load_kernel(token_ref, *refs):
    count = len(refs) // 2 - 1
    next_ref, *out_refs = refs[count:-1]
    copies = [
        pltpu.make_async_copy(ref, out_ref, refs[-1].at[k])
        for k, (ref, out_ref) in enumerate(zip(refs[:count], out_refs))
    ]
    for copy in copies:
        copy.start()
    next_ref[...] = token_ref[...]
    for copy in copies:
        copy.wait()


def load(token, *arrays):
    whole = pl.BlockSpec(memory_space=pltpu.VMEM)
    place = pl.BlockSpec(memory_space=pl.ANY)
    return pl.pallas_call(
        load_kernel,
        out_shape=[jax.ShapeDtypeStruct(x.shape, x.dtype) for x in (token, *arrays)],
        in_specs=[whole] + [place] * len(arrays),
        out_specs=[whole] * (1 + len(arrays)),
        scratch_shapes=[pltpu.SemaphoreType.DMA((len(arrays),))],
        compiler_params=pltpu.CompilerParams(vmem_limit_bytes=1 << 20),
        cost_estimate=pl.CostEstimate(flops=1, bytes_accessed=1, transcendentals=0),
        name="load",
    )(token, *arrays)


def ring_orders(devices):
    chips = devices // 2
    order = [2 * r if r < chips // 2 else 2 * (chips - 1 - r) + 1 for r in range(chips)]
    forward = [
        (2 * order[r] + core, 2 * order[(r + 1) % chips] + core)
        for r in range(chips)
        for core in range(2)
    ]
    backward = [(b, a) for a, b in forward]
    swap = [(i, i ^ 1) for i in range(devices)]
    return forward, backward, swap


def fence_kernel(token_ref, *refs):
    refs[len(refs) // 2][...] = token_ref[...]


def fence(token, values):
    place = pl.BlockSpec(memory_space=pl.ANY)
    whole = pl.BlockSpec(memory_space=pltpu.VMEM)
    token, *values = pl.pallas_call(
        fence_kernel,
        out_shape=[jax.ShapeDtypeStruct(x.shape, x.dtype) for x in (token, *values)],
        in_specs=[whole] + [place] * len(values),
        out_specs=[whole] + [place] * len(values),
        input_output_aliases={k: k for k in range(1, len(values) + 1)},
        compiler_params=pltpu.CompilerParams(vmem_limit_bytes=1 << 20),
        cost_estimate=pl.CostEstimate(flops=1, bytes_accessed=4 << 20, transcendentals=0),
        name="fence",
    )(token, *values)
    return token, values


def merge_kernel(token_ref, ahead_terms, behind_terms, *refs, cuts):
    *moving, next_ref, ahead_ref, behind_ref = refs
    next_ref[...] = token_ref[...]
    for way, (terms_ref, out_ref) in enumerate(
        ((ahead_terms, ahead_ref), (behind_terms, behind_ref))
    ):
        total = terms_ref[cuts[way]]
        if moving:
            total = (total.astype(F32) + moving[way][...].astype(F32)).astype(BF16)
        out_ref[...] = total


def merge(token, terms, cuts, moving):
    whole = pl.BlockSpec(memory_space=pltpu.VMEM)
    part = jax.ShapeDtypeStruct((cuts[0].stop - cuts[0].start, terms[0].shape[1]), BF16)
    return pl.pallas_call(
        functools.partial(merge_kernel, cuts=cuts),
        out_shape=[jax.ShapeDtypeStruct(token.shape, token.dtype), part, part],
        in_specs=[whole] * (3 + len(moving)),
        out_specs=[whole] * 3,
        compiler_params=pltpu.CompilerParams(vmem_limit_bytes=4 << 20),
        cost_estimate=pl.CostEstimate(flops=1, bytes_accessed=1, transcendentals=0),
        name="merge",
    )(token, *terms, *moving)


def finish_kernel(terms_ref, *refs):
    *sum_refs, out_ref = refs
    batches, tokens, model_width = out_ref.shape
    stream_refs, sum_refs = sum_refs[:batches], sum_refs[batches:]
    half = model_width // batches
    for side in range(2):
        total = terms_ref[side * tokens : (side + 1) * tokens].astype(F32)
        for sum_ref in sum_refs[2 * side : 2 * side + 2]:
            total = total + sum_ref[...].astype(F32)
        cols = slice(side * half, (side + 1) * half)
        for batch, stream_ref in enumerate(stream_refs):
            came = total[:, batch * half : (batch + 1) * half]
            out_ref[batch, :, cols] = (stream_ref[:, cols] + came).astype(BF16)


def finish(terms, streams, sums):
    whole = pl.BlockSpec(memory_space=pltpu.VMEM)
    return pl.pallas_call(
        finish_kernel,
        out_shape=jax.ShapeDtypeStruct((len(streams), *streams[0].shape), BF16),
        in_specs=[whole] * (1 + len(streams) + len(sums)),
        out_specs=whole,
        compiler_params=pltpu.CompilerParams(vmem_limit_bytes=8 << 20),
        name="finish",
    )(terms, *streams, *sums)


class Line:
    def __init__(self):
        self.token = jnp.zeros((16, 128), F32)

    def hold(self, values):
        self.token, values = fence(self.token, values)
        return values


def body(queries, keys_values, residual, norm_gain, gate_up, down_proj, expert_ids, expert_gates):
    devices = lax.axis_size("dev")
    batches, tokens, model_width = residual.shape
    length, feat_width = queries.shape[2:]
    kv_heads = model_width // feat_width
    forward, backward, swap = ring_orders(devices)
    chips = devices // 2
    reach = chips // 2
    half = model_width // 2
    me = lax.axis_index("dev").astype(jnp.int32).reshape(1)
    me, queries = lax.optimization_barrier((me, queries))
    send_ahead = lambda x: lax.ppermute(x, "dev", forward)
    send_behind = lambda x: lax.ppermute(x, "dev", backward)
    swapped = lambda x: lax.ppermute(x, "dev", swap)
    line = Line()

    gate_up_b, down_b = swapped(gate_up), swapped(down_proj)
    rows = attend(queries, keys_values, expert_ids, expert_gates, devices)
    arrived = lax.all_to_all(
        rows.reshape(devices, -1, rows.shape[-1]), "dev", split_axis=0, concat_axis=0, tiled=True
    )
    arrived, gate_up_b, down_b = line.hold([arrived, gate_up_b, down_b])
    arrived = arrived.reshape(rows.shape)
    left, right, streams = prepare(arrived, residual, norm_gain, kv_heads)
    shares = arrived[:, 0, 0, feat_width:].astype(F32) + arrived[:, 0, 1, feat_width:].astype(F32)
    shares = [shares, swapped(shares)]

    class Chain:
        def __init__(self, ahead, behind):
            self.moving = [ahead, behind]

        def send(self):
            self.moving = [send_ahead(self.moving[0]), send_behind(self.moving[1])]

        def land(self):
            self.moving = line.hold(self.moving)

    long, short = Chain(left, right), Chain(right, left)
    held = {0: [left, right]}
    terms = {}

    def experts(*places):
        blocks = [block for place in places for block in held[place]]
        out, line.token = run_experts(me, line.token, shares, weights, blocks, places)
        for k, place in enumerate(places):
            terms[place] = (out, 2 * k * tokens)

    def send_back(chain, step, first=False):
        pairs = ((step, 0), (-step % chips, 1)) if chain is long else ((step, 1), (-step % chips, 0))
        outs, cuts = [], []
        for place, side in pairs:
            out, row = terms[place]
            outs.append(out)
            cuts.append(slice(row + side * tokens, row + (side + 1) * tokens))
        line.token, *chain.moving = merge(line.token, outs, cuts, [] if first else chain.moving)
        chain.send()

    short.send()
    long.send()
    line.token, gate_up_b = load(line.token, gate_up_b)
    weights = [gate_up, gate_up_b, down_proj, down_b]
    for step in range(1, reach):
        short.land()
        came_right, came_left = short.moving
        if step < reach - 1:
            short.send()
        if step == 2:
            experts(chips - 1)
        long.land()
        held[step] = [came_left, long.moving[1]]
        held[chips - step] = [long.moving[0], came_right]
        long.send()
        if step == 1:
            experts(1)
        else:
            experts(step, chips - step)
    send_back(short, reach - 1, True)
    long.land()
    held[reach] = long.moving
    experts(reach)
    send_back(long, reach, True)
    for step in range(reach - 2, 0, -1):
        send_back(short, step)
        send_back(long, step + 1)
        if step == 1:
            experts(0)
    short.land()
    send_back(long, 1)
    ahead, behind = long.moving
    short_ahead, short_behind = short.moving
    return finish(terms[0][0], streams, [ahead, short_behind, behind, short_ahead])


def solution(mesh):
    in_specs = (
        P(None, ("groups", "dev"), None, None),
        P(None, ("groups", "dev"), None, None, None),
        P(None, ("groups", "dev"), None),
        P(),
        P("dev", None, None),
        P("dev", None, None),
        P(None, ("groups", "dev"), None),
        P(None, ("groups", "dev"), None),
    )
    out_specs = P(None, ("groups", "dev"), None)
    return jax.shard_map(body, mesh=mesh, in_specs=in_specs, out_specs=out_specs, check_vma=False)
```

```python
import functools
import math

import jax
import jax.numpy as jnp
import numpy as np
from jax import lax
from jax.experimental import pallas as pl
from jax.experimental.pallas import tpu as pltpu
from jax.sharding import PartitionSpec as P

F32 = jnp.float32
BF16 = jnp.bfloat16


def attend_kernel(q_ref, kv_ref, ids_ref, gates_ref, out_ref, values_ref, *, devices):
    length, feat_width = q_ref.shape
    context, head_size = kv_ref.shape[1:]
    positions = length // devices
    scale = math.log2(math.e) / math.sqrt(head_size)
    keys = kv_ref[0]
    values_ref[:, :head_size] = kv_ref[1]
    values_ref[:, head_size:] = jnp.ones((context, head_size), BF16)
    row = lax.broadcasted_iota(jnp.int32, (length, length), 0)
    col = lax.broadcasted_iota(jnp.int32, (length, length), 1)
    heads = feat_width // head_size
    stack = 2 if heads % 2 == 0 else 1
    allowed = jnp.concatenate([col <= row] * stack, axis=0)

    def put(cols, value):
        if len(out_ref.shape) == 3:
            value = value.reshape(devices, positions, value.shape[-1])
            out_ref[:, :, cols] = value.astype(BF16)
        else:
            out_ref[:, cols] = value.astype(BF16)

    for first in range(0, heads, stack):
        cols = [slice(h * head_size, (h + 1) * head_size) for h in range(first, first + stack)]
        scores = lax.dot_general(
            jnp.concatenate([q_ref[:, c] for c in cols], axis=0),
            keys,
            (((1,), (1,)), ((), ())),
            preferred_element_type=F32,
        )
        cached = scores[:, : context - length]
        fresh = jnp.where(allowed, scores[:, context - length :], -1e30)
        highest = jnp.maximum(
            jnp.max(cached, axis=-1, keepdims=True), jnp.max(fresh, axis=-1, keepdims=True)
        )
        grown = jnp.concatenate(
            [jnp.exp2((cached - highest) * scale), jnp.exp2((fresh - highest) * scale)], axis=1
        )
        both = jnp.dot(grown.astype(BF16), values_ref[...], preferred_element_type=F32)
        blended = both[:, :head_size] / both[:, head_size:]
        for k, c in enumerate(cols):
            put(c, blended[k * length : (k + 1) * length])

    batches, top, tokens = ids_ref.shape
    lines = batches * tokens
    last = slice(feat_width, feat_width + lines)
    tables = []
    for batch in range(batches):
        shares = gates_ref[batch].astype(F32)
        shares = shares / jnp.sum(shares, axis=0, keepdims=True)
        expert = lax.broadcasted_iota(jnp.int32, (devices, tokens), 0)
        table = jnp.zeros((devices, tokens), F32)
        for k in range(top):
            named = expert == ids_ref[batch, k : k + 1]
            table += jnp.where(named, shares[k : k + 1], 0.0)
        tables.append(table)
    table = jnp.concatenate(tables, axis=1)
    high = table.astype(BF16).astype(F32)
    part = lax.broadcasted_iota(jnp.int32, (devices, positions, lines), 1)
    spread = [jnp.broadcast_to(x[:, None, :], part.shape) for x in (high, table - high)]
    both = jnp.where(part == 0, spread[0], jnp.where(part == 1, spread[1], 0.0))
    put(last, both.reshape(length, lines))


def attend(queries, keys_values, expert_ids, expert_gates, devices):
    batches, _, length, feat_width = queries.shape
    context, head_size = keys_values.shape[3:]
    positions = length // devices
    pairs = batches * length * (feat_width // head_size) * context
    queries, keys_values, *choices = [
        pltpu.with_memory_space_constraint(x, pltpu.HBM)
        for x in (
            queries,
            keys_values,
            jnp.swapaxes(expert_ids, 1, 2),
            jnp.swapaxes(expert_gates, 1, 2),
        )
    ]
    width = feat_width + batches * expert_ids.shape[1]
    direct = positions % 8 == 0
    if direct:
        shape = (devices, batches, positions, width)
        out_spec = pl.BlockSpec((devices, None, positions, width), lambda i: (0, i, 0, 0))
    else:
        shape = (batches, length, width)
        out_spec = pl.BlockSpec((None, length, width), lambda i: (i, 0, 0))
    rows = pl.pallas_call(
        functools.partial(attend_kernel, devices=devices),
        out_shape=jax.ShapeDtypeStruct(shape, BF16),
        grid=(batches,),
        in_specs=[
            pl.BlockSpec((None, None, length, feat_width), lambda i: (i, 0, 0, 0)),
            pl.BlockSpec((None, None, 2, context, head_size), lambda i: (i, 0, 0, 0, 0)),
        ]
        + [pl.BlockSpec(c.shape, lambda i: (0, 0, 0)) for c in choices],
        out_specs=out_spec,
        scratch_shapes=[pltpu.VMEM((context, 2 * head_size), BF16)],
        compiler_params=pltpu.CompilerParams(vmem_limit_bytes=24 << 20),
        cost_estimate=pl.CostEstimate(
            flops=4 * pairs * head_size,
            bytes_accessed=2 * batches * (2 * length * feat_width + 2 * context * head_size),
            transcendentals=pairs,
        ),
        name="attend",
    )(queries, keys_values, *choices)
    if not direct:
        rows = jnp.swapaxes(rows.reshape(batches, devices, positions, width), 0, 1)
    return rows


def prepare_kernel(arrived_ref, residual_ref, gain_ref, left_ref, right_ref, *stream_refs, kv_heads):
    batches, tokens, model_width = residual_ref.shape
    feat_width = model_width // kv_heads
    half = model_width // batches
    for batch, stream_ref in enumerate(stream_refs):
        if len(arrived_ref.shape) == 4:
            sources, _, positions, _ = arrived_ref.shape
            for source in range(sources):
                first = source // kv_heads * positions
                left = source % kv_heads * feat_width
                stream_ref[first : first + positions, left : left + feat_width] = arrived_ref[
                    source, batch, :, :feat_width
                ].astype(F32)
            rows = stream_ref[...]
        else:
            rows = arrived_ref[batch].astype(F32)
        stream = residual_ref[batch].astype(F32) + rows
        stream_ref[...] = stream
        meansq = jnp.mean(stream * stream, axis=-1, keepdims=True)
        own = (stream * lax.rsqrt(meansq + 1e-06) * gain_ref[...]).astype(BF16)
        left_ref[:, batch * half : (batch + 1) * half] = own[:, :half]
        right_ref[:, batch * half : (batch + 1) * half] = own[:, half:]


def prepare(arrived, residual, norm_gain, kv_heads):
    batches, tokens, model_width = residual.shape
    sources, _, positions, _ = arrived.shape
    feat_width = model_width // kv_heads
    if positions % 8:
        rows = arrived[..., :feat_width]
        rows = rows.reshape(sources // kv_heads, kv_heads, batches, positions, feat_width)
        arrived = jnp.transpose(rows, (2, 0, 3, 1, 4)).reshape(batches, tokens, model_width)
    row = (tokens, model_width)
    whole = pl.BlockSpec(memory_space=pltpu.VMEM)
    left, right, *streams = pl.pallas_call(
        functools.partial(prepare_kernel, kv_heads=kv_heads),
        out_shape=[jax.ShapeDtypeStruct(row, BF16)] * 2
        + [jax.ShapeDtypeStruct(row, F32)] * batches,
        in_specs=[whole] * 3,
        out_specs=[whole] * (2 + batches),
        compiler_params=pltpu.CompilerParams(vmem_limit_bytes=8 << 20),
        name="prepare",
    )(arrived, residual, norm_gain.reshape(1, model_width))
    return left, right, streams


def ring_place(device, step, devices):
    chips = devices // 2
    chip, core = device // 2, device % 2
    place = jnp.where(chip % 2 == 0, chip // 2, chips - 1 - chip // 2)
    place = (place + step) % chips
    chip = jnp.where(place < chips // 2, 2 * place, 2 * (chips - 1 - place) + 1)
    return 2 * chip + core


def pre_activations(x_ref, gate_up_ref, cols, sides, blocks):
    if sides is None:
        return jnp.dot(x_ref[...], gate_up_ref[0, :, cols], preferred_element_type=F32)
    rows, half = x_ref.shape
    rows = rows // blocks
    parts = []
    for block, side in enumerate(sides):
        parts.append(
            jnp.dot(
                x_ref[block * rows : (block + 1) * rows],
                gate_up_ref[0, side * half : (side + 1) * half, cols],
                preferred_element_type=F32,
            )
        )
    return jnp.concatenate(parts, axis=0)


def gather_halves(x_ref, half_refs):
    tokens, width = half_refs[0].shape
    for block, ref in enumerate(half_refs):
        for batch in range(2):
            row = (2 * block + batch) * tokens
            came = slice(batch * width // 2, (batch + 1) * width // 2)
            x_ref[row : row + tokens] = ref[:, came]


def begin_kernel(token_ref, gate_up_a, gate_up_b, *refs, sides):
    *half_refs, pre_a, pre_b, next_ref, x_ref = refs
    next_ref[...] = token_ref[...]
    gather_halves(x_ref, half_refs)
    for gate_up_ref, pre_ref in ((gate_up_a, pre_a), (gate_up_b, pre_b)):
        width = pre_ref.shape[1]
        part = min(256, width)
        for start in range(0, width, part):
            cols = slice(start, start + part)
            pre_ref[:, cols] = pre_activations(x_ref, gate_up_ref, cols, sides, len(half_refs))


def begin_experts(token, weights, halves, sides):
    tokens, width = halves[0].shape
    rows = 2 * tokens * len(halves)
    hidden = weights[0].shape[2]
    whole = pl.BlockSpec(memory_space=pltpu.VMEM)
    return pl.pallas_call(
        functools.partial(begin_kernel, sides=sides),
        out_shape=[jax.ShapeDtypeStruct((rows, hidden), F32)] * 2
        + [jax.ShapeDtypeStruct(token.shape, token.dtype)],
        in_specs=[whole] * (3 + len(halves)),
        out_specs=[whole] * 3,
        scratch_shapes=[pltpu.VMEM((rows, width // 2), BF16)],
        compiler_params=pltpu.CompilerParams(vmem_limit_bytes=8 << 20),
        cost_estimate=pl.CostEstimate(flops=1, bytes_accessed=1, transcendentals=0),
        name="begin",
    )(token, *weights[:2], *halves)


def expert_kernel(
    me_ref, token_ref, share_a, share_b, gate_up_a, gate_up_b, down_a, down_b, *refs, places, sides
):
    *held_refs, out_ref, next_ref, x_all, hidden_a, hidden_b = refs
    next_ref[...] = token_ref[...]
    begun = (None, None)
    if sides is not None:
        *held_refs, pre_a, pre_b = held_refs
        begun = (pre_a, pre_b)
    tokens, model_width = held_refs[0].shape
    half = model_width // 2
    blocks = len(places)
    hidden_width = down_a.shape[1]
    devices, lanes = share_a.shape
    part = min(256, hidden_width)
    chunk = min(512, half)

    row_of = lambda block, batch: (block * 2 + batch) * tokens
    if sides is not None:
        gather_halves(x_all, held_refs)
    else:
        for block in range(blocks):
            for side in range(2):
                cols = slice(side * half, (side + 1) * half)
                for batch in range(2):
                    row = row_of(block, batch)
                    came = slice(batch * half, (batch + 1) * half)
                    x_all[row : row + tokens, cols] = held_refs[2 * block + side][:, came]
    token = lax.broadcasted_iota(jnp.int32, (tokens, lanes), 0)
    lane = lax.broadcasted_iota(jnp.int32, (tokens, lanes), 1)
    for share_ref, gate_up_ref, hidden_ref, pre_ref in (
        (share_a, gate_up_a, hidden_a, begun[0]),
        (share_b, gate_up_b, hidden_b, begun[1]),
    ):
        shares = []
        for place in places:
            source = ring_place(me_ref[0], place, devices)
            line = jnp.broadcast_to(share_ref[pl.ds(source, 1), :], (tokens, lanes))
            for batch in range(2):
                spread = jnp.where(lane == token + batch * tokens, line, 0.0)
                shares.append(jnp.sum(spread, axis=-1, keepdims=True))
        share = jnp.concatenate(shares, axis=0)
        for start in range(0, hidden_width, part):
            pair = []
            for first in (start, hidden_width + start):
                cols = slice(first, first + part)
                pre = pre_activations(x_all, gate_up_ref, cols, sides, blocks)
                pair.append(pre if pre_ref is None else pre + pre_ref[:, cols])
            gate, up = pair
            act = gate / (1.0 + jnp.exp(-gate)) * up
            hidden_ref[:, start : start + part] = (act * share).astype(BF16)
    for start in range(0, model_width, chunk):
        cols = slice(start, start + chunk)
        total = jnp.dot(hidden_a[...], down_a[0, :, cols], preferred_element_type=F32)
        total += jnp.dot(hidden_b[...], down_b[0, :, cols], preferred_element_type=F32)
        weighted = total.astype(BF16)
        side, left = start // half, start % half
        for block in range(blocks):
            rows = slice((2 * block + side) * tokens, (2 * block + side + 1) * tokens)
            for batch in range(2):
                row = row_of(block, batch)
                goes = slice(batch * half + left, batch * half + left + chunk)
                out_ref[rows, goes] = weighted[row : row + tokens]


def run_experts(me, token, shares, weights, held, places, sides=None, begun=()):
    tokens, model_width = held[0].shape
    rows = 2 * tokens * len(places)
    hidden_width = weights[2].shape[1]
    whole = pl.BlockSpec(memory_space=pltpu.VMEM)
    return pl.pallas_call(
        functools.partial(expert_kernel, places=places, sides=sides),
        out_shape=[
            jax.ShapeDtypeStruct((rows, model_width), BF16),
            jax.ShapeDtypeStruct(token.shape, token.dtype),
        ],
        in_specs=[pl.BlockSpec(memory_space=pltpu.SMEM)] + [whole] * (7 + len(held) + len(begun)),
        out_specs=[whole] * 2,
        scratch_shapes=[
            pltpu.VMEM((rows, model_width if sides is None else model_width // 2), BF16),
            pltpu.VMEM((rows, hidden_width), BF16),
            pltpu.VMEM((rows, hidden_width), BF16),
        ],
        compiler_params=pltpu.CompilerParams(vmem_limit_bytes=10 << 20),
        cost_estimate=pl.CostEstimate(flops=1, bytes_accessed=1, transcendentals=0),
        name="experts",
    )(me, token, *shares, *weights, *held, *begun)


def load_kernel(token_ref, *refs):
    count = len(refs) // 2 - 1
    next_ref, *out_refs = refs[count:-1]
    copies = [
        pltpu.make_async_copy(ref, out_ref, refs[-1].at[k])
        for k, (ref, out_ref) in enumerate(zip(refs[:count], out_refs))
    ]
    for copy in copies:
        copy.start()
    next_ref[...] = token_ref[...]
    for copy in copies:
        copy.wait()


def load(token, *arrays):
    whole = pl.BlockSpec(memory_space=pltpu.VMEM)
    place = pl.BlockSpec(memory_space=pl.ANY)
    return pl.pallas_call(
        load_kernel,
        out_shape=[jax.ShapeDtypeStruct(x.shape, x.dtype) for x in (token, *arrays)],
        in_specs=[whole] + [place] * len(arrays),
        out_specs=[whole] * (1 + len(arrays)),
        scratch_shapes=[pltpu.SemaphoreType.DMA((len(arrays),))],
        compiler_params=pltpu.CompilerParams(vmem_limit_bytes=1 << 20),
        cost_estimate=pl.CostEstimate(flops=1, bytes_accessed=1, transcendentals=0),
        name="load",
    )(token, *arrays)


def ring_orders(devices):
    chips = devices // 2
    order = [2 * r if r < chips // 2 else 2 * (chips - 1 - r) + 1 for r in range(chips)]
    forward = [
        (2 * order[r] + core, 2 * order[(r + 1) % chips] + core)
        for r in range(chips)
        for core in range(2)
    ]
    backward = [(b, a) for a, b in forward]
    swap = [(i, i ^ 1) for i in range(devices)]
    return forward, backward, swap


def fence_kernel(token_ref, *refs):
    refs[len(refs) // 2][...] = token_ref[...]


def fence(token, values):
    place = pl.BlockSpec(memory_space=pl.ANY)
    whole = pl.BlockSpec(memory_space=pltpu.VMEM)
    token, *values = pl.pallas_call(
        fence_kernel,
        out_shape=[jax.ShapeDtypeStruct(x.shape, x.dtype) for x in (token, *values)],
        in_specs=[whole] + [place] * len(values),
        out_specs=[whole] + [place] * len(values),
        input_output_aliases={k: k for k in range(1, len(values) + 1)},
        compiler_params=pltpu.CompilerParams(vmem_limit_bytes=1 << 20),
        cost_estimate=pl.CostEstimate(flops=1, bytes_accessed=4 << 20, transcendentals=0),
        name="fence",
    )(token, *values)
    return token, values


def merge_kernel(token_ref, ahead_terms, behind_terms, *refs, cuts):
    *moving, next_ref, ahead_ref, behind_ref = refs
    next_ref[...] = token_ref[...]
    for way, (terms_ref, out_ref) in enumerate(
        ((ahead_terms, ahead_ref), (behind_terms, behind_ref))
    ):
        total = terms_ref[cuts[way]]
        if moving:
            total = (total.astype(F32) + moving[way][...].astype(F32)).astype(BF16)
        out_ref[...] = total


def merge(token, terms, cuts, moving):
    whole = pl.BlockSpec(memory_space=pltpu.VMEM)
    part = jax.ShapeDtypeStruct((cuts[0].stop - cuts[0].start, terms[0].shape[1]), BF16)
    return pl.pallas_call(
        functools.partial(merge_kernel, cuts=cuts),
        out_shape=[jax.ShapeDtypeStruct(token.shape, token.dtype), part, part],
        in_specs=[whole] * (3 + len(moving)),
        out_specs=[whole] * 3,
        compiler_params=pltpu.CompilerParams(vmem_limit_bytes=4 << 20),
        cost_estimate=pl.CostEstimate(flops=1, bytes_accessed=1, transcendentals=0),
        name="merge",
    )(token, *terms, *moving)


def finish_kernel(token_ref, terms_ref, *refs):
    *sum_refs, out_ref, rows_ref, sems = refs
    batches, tokens, model_width = rows_ref.shape
    stream_refs, sum_refs = sum_refs[:batches], sum_refs[batches:]
    half = model_width // batches
    copies = []
    for batch, stream_ref in enumerate(stream_refs):
        came = slice(batch * half, (batch + 1) * half)
        for side in range(2):
            cols = slice(side * half, (side + 1) * half)
            total = terms_ref[side * tokens : (side + 1) * tokens, came].astype(F32)
            for sum_ref in sum_refs[2 * side : 2 * side + 2]:
                total = total + sum_ref[:, came].astype(F32)
            rows_ref[batch, :, cols] = (stream_ref[:, cols] + total).astype(BF16)
        copies.append(pltpu.make_async_copy(rows_ref.at[batch], out_ref.at[batch], sems.at[batch]))
        copies[-1].start()
    for copy in copies:
        copy.wait()


def finish(token, terms, streams, sums):
    whole = pl.BlockSpec(memory_space=pltpu.VMEM)
    shape = (len(streams), *streams[0].shape)
    return pl.pallas_call(
        finish_kernel,
        out_shape=jax.ShapeDtypeStruct(shape, BF16),
        in_specs=[whole] * (2 + len(streams) + len(sums)),
        out_specs=pl.BlockSpec(memory_space=pl.ANY),
        scratch_shapes=[pltpu.VMEM(shape, BF16), pltpu.SemaphoreType.DMA((len(streams),))],
        compiler_params=pltpu.CompilerParams(vmem_limit_bytes=8 << 20),
        name="finish",
    )(token, terms, *streams, *sums)


class Line:
    def __init__(self):
        self.token = jnp.zeros((16, 128), F32)

    def hold(self, values):
        self.token, values = fence(self.token, values)
        return values


def body(queries, keys_values, residual, norm_gain, gate_up, down_proj, expert_ids, expert_gates):
    devices = lax.axis_size("dev")
    batches, tokens, model_width = residual.shape
    length, feat_width = queries.shape[2:]
    kv_heads = model_width // feat_width
    forward, backward, swap = ring_orders(devices)
    chips = devices // 2
    reach = chips // 2
    half = model_width // 2
    me = lax.axis_index("dev").astype(jnp.int32).reshape(1)
    me, queries = lax.optimization_barrier((me, queries))
    send_ahead = lambda x: lax.ppermute(x, "dev", forward)
    send_behind = lambda x: lax.ppermute(x, "dev", backward)
    swapped = lambda x: lax.ppermute(x, "dev", swap)
    line = Line()

    gate_up_b, down_b = swapped(gate_up), swapped(down_proj)
    rows = attend(queries, keys_values, expert_ids, expert_gates, devices)
    arrived = lax.all_to_all(
        rows.reshape(devices, -1, rows.shape[-1]), "dev", split_axis=0, concat_axis=0, tiled=True
    )
    arrived, gate_up_b, down_b = line.hold([arrived, gate_up_b, down_b])
    arrived = arrived.reshape(rows.shape)
    left, right, streams = prepare(arrived, residual, norm_gain, kv_heads)
    shares = arrived[:, 0, 0, feat_width:].astype(F32) + arrived[:, 0, 1, feat_width:].astype(F32)
    shares = [shares, swapped(shares)]

    class Chain:
        def __init__(self, ahead, behind):
            self.moving = [ahead, behind]

        def send(self):
            self.moving = [send_ahead(self.moving[0]), send_behind(self.moving[1])]

        def land(self):
            self.moving = line.hold(self.moving)

    long, short = Chain(left, right), Chain(right, left)
    held = {0: [left, right]}
    terms = {}

    def experts(*places):
        blocks = [block for place in places for block in held[place]]
        out, line.token = run_experts(me, line.token, shares, weights, blocks, places)
        for k, place in enumerate(places):
            terms[place] = (out, 2 * k * tokens)

    def send_back(chain, step, first=False):
        pairs = ((step, 0), (-step % chips, 1)) if chain is long else ((step, 1), (-step % chips, 0))
        outs, cuts = [], []
        for place, side in pairs:
            out, row = terms[place]
            outs.append(out)
            cuts.append(slice(row + side * tokens, row + (side + 1) * tokens))
        line.token, *chain.moving = merge(line.token, outs, cuts, [] if first else chain.moving)
        chain.send()

    long.send()
    short.send()
    line.token, gate_up_b = load(line.token, gate_up_b)
    weights = [gate_up, gate_up_b, down_proj, down_b]
    for step in range(1, reach):
        long.land()
        from_behind, from_ahead = long.moving
        long.send()
        if step == reach - 1:
            *begun, line.token = begin_experts(
                line.token, weights, [from_ahead, from_behind], (1, 0)
            )
        elif step == 2:
            experts(chips - 1)
        short.land()
        held[step] = [short.moving[1], from_ahead]
        held[chips - step] = [from_behind, short.moving[0]]
        if step < reach - 1:
            short.send()
        if step == reach - 1:
            places = (step, chips - step)
            out, line.token = run_experts(
                me, line.token, shares, weights, short.moving[::-1], places, (0, 1), begun
            )
            terms.update({place: (out, 2 * k * tokens) for k, place in enumerate(places)})
        elif step == 1:
            experts(1)
        else:
            experts(step, chips - step)
    if reach < 4:
        experts(chips - 1)
    send_back(short, reach - 1, True)
    long.land()
    held[reach] = long.moving
    experts(reach)
    send_back(long, reach, True)
    for step in range(reach - 2, 0, -1):
        send_back(short, step)
        send_back(long, step + 1)
        if step == 1:
            experts(0)
    short.land()
    send_back(long, 1)
    ahead, behind = long.moving
    short_ahead, short_behind = short.moving
    return finish(
        line.token, terms[0][0], streams, [ahead, short_behind, behind, short_ahead]
    )


def solution(mesh):
    in_specs = (
        P(None, ("groups", "dev"), None, None),
        P(None, ("groups", "dev"), None, None, None),
        P(None, ("groups", "dev"), None),
        P(),
        P("dev", None, None),
        P("dev", None, None),
        P(None, ("groups", "dev"), None),
        P(None, ("groups", "dev"), None),
    )
    out_specs = P(None, ("groups", "dev"), None)
    return jax.shard_map(body, mesh=mesh, in_specs=in_specs, out_specs=out_specs, check_vma=False)
```

```python
import functools
import math

import jax
import jax.numpy as jnp
import numpy as np
from jax import lax
from jax.experimental import pallas as pl
from jax.experimental.pallas import tpu as pltpu
from jax.sharding import PartitionSpec as P

F32 = jnp.float32
BF16 = jnp.bfloat16


def attend_kernel(q_ref, kv_ref, ids_ref, gates_ref, out_ref, values_ref, *, devices):
    length, feat_width = q_ref.shape
    context, head_size = kv_ref.shape[1:]
    positions = length // devices
    scale = math.log2(math.e) / math.sqrt(head_size)
    keys = kv_ref[0]
    values_ref[:, :head_size] = kv_ref[1]
    values_ref[:, head_size:] = jnp.ones((context, head_size), BF16)
    row = lax.broadcasted_iota(jnp.int32, (length, length), 0)
    col = lax.broadcasted_iota(jnp.int32, (length, length), 1)
    heads = feat_width // head_size
    stack = next(k for k in (4, 2, 1) if heads % k == 0)
    allowed = jnp.concatenate([col <= row] * stack, axis=0)

    def put(cols, value):
        if len(out_ref.shape) == 3:
            value = value.reshape(devices, positions, value.shape[-1])
            out_ref[:, :, cols] = value.astype(BF16)
        else:
            out_ref[:, cols] = value.astype(BF16)

    for first in range(0, heads, stack):
        cols = [slice(h * head_size, (h + 1) * head_size) for h in range(first, first + stack)]
        scores = lax.dot_general(
            jnp.concatenate([q_ref[:, c] for c in cols], axis=0),
            keys,
            (((1,), (1,)), ((), ())),
            preferred_element_type=F32,
        )
        cached = scores[:, : context - length]
        fresh = jnp.where(allowed, scores[:, context - length :], -1e30)
        highest = jnp.maximum(
            jnp.max(cached, axis=-1, keepdims=True), jnp.max(fresh, axis=-1, keepdims=True)
        )
        grown = jnp.concatenate(
            [jnp.exp2((cached - highest) * scale), jnp.exp2((fresh - highest) * scale)], axis=1
        )
        both = jnp.dot(grown.astype(BF16), values_ref[...], preferred_element_type=F32)
        blended = both[:, :head_size] / both[:, head_size:]
        for k, c in enumerate(cols):
            put(c, blended[k * length : (k + 1) * length])

    batches, top, tokens = ids_ref.shape
    lines = batches * tokens
    last = slice(feat_width, feat_width + lines)

    @pl.when(pl.program_id(0) == 0)
    def _():
        tables = []
        for batch in range(batches):
            shares = gates_ref[batch].astype(F32)
            shares = shares / jnp.sum(shares, axis=0, keepdims=True)
            expert = lax.broadcasted_iota(jnp.int32, (devices, tokens), 0)
            table = jnp.zeros((devices, tokens), F32)
            for k in range(top):
                named = expert == ids_ref[batch, k : k + 1]
                table += jnp.where(named, shares[k : k + 1], 0.0)
            tables.append(table)
        table = jnp.concatenate(tables, axis=1)
        high = table.astype(BF16).astype(F32)
        part = lax.broadcasted_iota(jnp.int32, (devices, positions, lines), 1)
        spread = [jnp.broadcast_to(x[:, None, :], part.shape) for x in (high, table - high)]
        both = jnp.where(part == 0, spread[0], jnp.where(part == 1, spread[1], 0.0))
        put(last, both.reshape(length, lines))

    @pl.when(pl.program_id(0) > 0)
    def _():
        put(last, jnp.zeros((length, lines), F32))


def attend(queries, keys_values, expert_ids, expert_gates, devices):
    batches, _, length, feat_width = queries.shape
    context, head_size = keys_values.shape[3:]
    positions = length // devices
    pairs = batches * length * (feat_width // head_size) * context
    queries, keys_values, *choices = [
        pltpu.with_memory_space_constraint(x, pltpu.HBM)
        for x in (
            queries,
            keys_values,
            jnp.swapaxes(expert_ids, 1, 2),
            jnp.swapaxes(expert_gates, 1, 2),
        )
    ]
    width = feat_width + batches * expert_ids.shape[1]
    direct = positions % 8 == 0
    if direct:
        shape = (devices, batches, positions, width)
        out_spec = pl.BlockSpec((devices, None, positions, width), lambda i: (0, i, 0, 0))
    else:
        shape = (batches, length, width)
        out_spec = pl.BlockSpec((None, length, width), lambda i: (i, 0, 0))
    rows = pl.pallas_call(
        functools.partial(attend_kernel, devices=devices),
        out_shape=jax.ShapeDtypeStruct(shape, BF16),
        grid=(batches,),
        in_specs=[
            pl.BlockSpec((None, None, length, feat_width), lambda i: (i, 0, 0, 0)),
            pl.BlockSpec((None, None, 2, context, head_size), lambda i: (i, 0, 0, 0, 0)),
        ]
        + [pl.BlockSpec(c.shape, lambda i: (0, 0, 0)) for c in choices],
        out_specs=out_spec,
        scratch_shapes=[pltpu.VMEM((context, 2 * head_size), BF16)],
        compiler_params=pltpu.CompilerParams(vmem_limit_bytes=14 << 20),
        cost_estimate=pl.CostEstimate(
            flops=4 * pairs * head_size,
            bytes_accessed=2 * batches * (2 * length * feat_width + 2 * context * head_size),
            transcendentals=pairs,
        ),
        name="attend",
    )(queries, keys_values, *choices)
    if not direct:
        rows = jnp.swapaxes(rows.reshape(batches, devices, positions, width), 0, 1)
    return rows


def prepare_kernel(arrived_ref, residual_ref, gain_ref, left_ref, right_ref, *stream_refs, kv_heads):
    batches, tokens, model_width = residual_ref.shape
    feat_width = model_width // kv_heads
    half = model_width // batches
    for batch, stream_ref in enumerate(stream_refs):
        if len(arrived_ref.shape) == 4:
            sources, _, positions, _ = arrived_ref.shape
            for source in range(sources):
                first = source // kv_heads * positions
                left = source % kv_heads * feat_width
                stream_ref[first : first + positions, left : left + feat_width] = arrived_ref[
                    source, batch, :, :feat_width
                ].astype(F32)
            rows = stream_ref[...]
        else:
            rows = arrived_ref[batch].astype(F32)
        stream = residual_ref[batch].astype(F32) + rows
        stream_ref[...] = stream
        meansq = jnp.mean(stream * stream, axis=-1, keepdims=True)
        own = (stream * lax.rsqrt(meansq + 1e-06) * gain_ref[...]).astype(BF16)
        left_ref[:, batch * half : (batch + 1) * half] = own[:, :half]
        right_ref[:, batch * half : (batch + 1) * half] = own[:, half:]


def prepare(arrived, residual, norm_gain, kv_heads):
    batches, tokens, model_width = residual.shape
    sources, _, positions, _ = arrived.shape
    feat_width = model_width // kv_heads
    if positions % 8:
        rows = arrived[..., :feat_width]
        rows = rows.reshape(sources // kv_heads, kv_heads, batches, positions, feat_width)
        arrived = jnp.transpose(rows, (2, 0, 3, 1, 4)).reshape(batches, tokens, model_width)
    row = (tokens, model_width)
    whole = pl.BlockSpec(memory_space=pltpu.VMEM)
    left, right, *streams = pl.pallas_call(
        functools.partial(prepare_kernel, kv_heads=kv_heads),
        out_shape=[jax.ShapeDtypeStruct(row, BF16)] * 2
        + [jax.ShapeDtypeStruct(row, F32)] * batches,
        in_specs=[whole] * 3,
        out_specs=[whole] * (2 + batches),
        compiler_params=pltpu.CompilerParams(vmem_limit_bytes=8 << 20),
        name="prepare",
    )(arrived, residual, norm_gain.reshape(1, model_width))
    return left, right, streams


def ring_place(device, step, devices):
    chips = devices // 2
    chip, core = device // 2, device % 2
    place = jnp.where(chip % 2 == 0, chip // 2, chips - 1 - chip // 2)
    place = (place + step) % chips
    chip = jnp.where(place < chips // 2, 2 * place, 2 * (chips - 1 - place) + 1)
    return 2 * chip + core


def pre_activations(x_ref, gate_up_ref, cols, sides, blocks):
    if sides is None:
        return jnp.dot(x_ref[...], gate_up_ref[0, :, cols], preferred_element_type=F32)
    rows, half = x_ref.shape
    rows = rows // blocks
    parts = []
    for block, side in enumerate(sides):
        parts.append(
            jnp.dot(
                x_ref[block * rows : (block + 1) * rows],
                gate_up_ref[0, side * half : (side + 1) * half, cols],
                preferred_element_type=F32,
            )
        )
    return jnp.concatenate(parts, axis=0)


def gather_halves(x_ref, half_refs):
    tokens, width = half_refs[0].shape
    for block, ref in enumerate(half_refs):
        for batch in range(2):
            row = (2 * block + batch) * tokens
            came = slice(batch * width // 2, (batch + 1) * width // 2)
            x_ref[row : row + tokens] = ref[:, came]


def begin_kernel(token_ref, gate_up_a, gate_up_b, *refs, sides):
    *half_refs, pre_a, pre_b, next_ref, x_ref = refs
    next_ref[...] = token_ref[...]
    gather_halves(x_ref, half_refs)
    for gate_up_ref, pre_ref in ((gate_up_a, pre_a), (gate_up_b, pre_b)):
        width = pre_ref.shape[1]
        part = min(256, width)
        for start in range(0, width, part):
            cols = slice(start, start + part)
            pre_ref[:, cols] = pre_activations(x_ref, gate_up_ref, cols, sides, len(half_refs))


def begin_experts(token, weights, halves, sides):
    tokens, width = halves[0].shape
    rows = 2 * tokens * len(halves)
    hidden = weights[0].shape[2]
    whole = pl.BlockSpec(memory_space=pltpu.VMEM)
    return pl.pallas_call(
        functools.partial(begin_kernel, sides=sides),
        out_shape=[jax.ShapeDtypeStruct((rows, hidden), F32)] * 2
        + [jax.ShapeDtypeStruct(token.shape, token.dtype)],
        in_specs=[whole] * (3 + len(halves)),
        out_specs=[whole] * 3,
        scratch_shapes=[pltpu.VMEM((rows, width // 2), BF16)],
        compiler_params=pltpu.CompilerParams(vmem_limit_bytes=8 << 20),
        cost_estimate=pl.CostEstimate(flops=1, bytes_accessed=1, transcendentals=0),
        name="begin",
    )(token, *weights[:2], *halves)


def expert_kernel(
    me_ref, token_ref, share_a, share_b, gate_up_a, gate_up_b, down_a, down_b, *refs, places, sides
):
    *held_refs, out_ref, next_ref, x_all, hidden_a, hidden_b = refs
    next_ref[...] = token_ref[...]
    begun = (None, None)
    if sides is not None:
        *held_refs, pre_a, pre_b = held_refs
        begun = (pre_a, pre_b)
    tokens, model_width = held_refs[0].shape
    half = model_width // 2
    blocks = len(places)
    hidden_width = down_a.shape[1]
    devices, lanes = share_a.shape
    part = min(256, hidden_width)
    chunk = min(512, half)

    row_of = lambda block, batch: (block * 2 + batch) * tokens
    if sides is not None:
        gather_halves(x_all, held_refs)
    else:
        for block in range(blocks):
            for side in range(2):
                cols = slice(side * half, (side + 1) * half)
                for batch in range(2):
                    row = row_of(block, batch)
                    came = slice(batch * half, (batch + 1) * half)
                    x_all[row : row + tokens, cols] = held_refs[2 * block + side][:, came]
    token = lax.broadcasted_iota(jnp.int32, (tokens, lanes), 0)
    lane = lax.broadcasted_iota(jnp.int32, (tokens, lanes), 1)
    for share_ref, gate_up_ref, hidden_ref, pre_ref in (
        (share_a, gate_up_a, hidden_a, begun[0]),
        (share_b, gate_up_b, hidden_b, begun[1]),
    ):
        shares = []
        for place in places:
            source = ring_place(me_ref[0], place, devices)
            line = jnp.broadcast_to(share_ref[pl.ds(source, 1), :], (tokens, lanes))
            for batch in range(2):
                spread = jnp.where(lane == token + batch * tokens, line, 0.0)
                shares.append(jnp.sum(spread, axis=-1, keepdims=True))
        share = jnp.concatenate(shares, axis=0)
        for start in range(0, hidden_width, part):
            pair = []
            for first in (start, hidden_width + start):
                cols = slice(first, first + part)
                pre = pre_activations(x_all, gate_up_ref, cols, sides, blocks)
                pair.append(pre if pre_ref is None else pre + pre_ref[:, cols])
            gate, up = pair
            act = gate / (1.0 + jnp.exp(-gate)) * up
            hidden_ref[:, start : start + part] = (act * share).astype(BF16)
    for start in range(0, model_width, chunk):
        cols = slice(start, start + chunk)
        total = jnp.dot(hidden_a[...], down_a[0, :, cols], preferred_element_type=F32)
        total += jnp.dot(hidden_b[...], down_b[0, :, cols], preferred_element_type=F32)
        weighted = total.astype(BF16)
        side, left = start // half, start % half
        for block in range(blocks):
            rows = slice((2 * block + side) * tokens, (2 * block + side + 1) * tokens)
            for batch in range(2):
                row = row_of(block, batch)
                goes = slice(batch * half + left, batch * half + left + chunk)
                out_ref[rows, goes] = weighted[row : row + tokens]


def run_experts(me, token, shares, weights, held, places, sides=None, begun=()):
    tokens, model_width = held[0].shape
    rows = 2 * tokens * len(places)
    hidden_width = weights[2].shape[1]
    whole = pl.BlockSpec(memory_space=pltpu.VMEM)
    return pl.pallas_call(
        functools.partial(expert_kernel, places=places, sides=sides),
        out_shape=[
            jax.ShapeDtypeStruct((rows, model_width), BF16),
            jax.ShapeDtypeStruct(token.shape, token.dtype),
        ],
        in_specs=[pl.BlockSpec(memory_space=pltpu.SMEM)] + [whole] * (7 + len(held) + len(begun)),
        out_specs=[whole] * 2,
        scratch_shapes=[
            pltpu.VMEM((rows, model_width if sides is None else model_width // 2), BF16),
            pltpu.VMEM((rows, hidden_width), BF16),
            pltpu.VMEM((rows, hidden_width), BF16),
        ],
        compiler_params=pltpu.CompilerParams(vmem_limit_bytes=10 << 20),
        cost_estimate=pl.CostEstimate(flops=1, bytes_accessed=1, transcendentals=0),
        name="experts",
    )(me, token, *shares, *weights, *held, *begun)


def load_kernel(token_ref, *refs):
    count = len(refs) // 2 - 1
    next_ref, *out_refs = refs[count:-1]
    copies = [
        pltpu.make_async_copy(ref, out_ref, refs[-1].at[k])
        for k, (ref, out_ref) in enumerate(zip(refs[:count], out_refs))
    ]
    for copy in copies:
        copy.start()
    next_ref[...] = token_ref[...]
    for copy in copies:
        copy.wait()


def load(token, *arrays):
    whole = pl.BlockSpec(memory_space=pltpu.VMEM)
    place = pl.BlockSpec(memory_space=pl.ANY)
    return pl.pallas_call(
        load_kernel,
        out_shape=[jax.ShapeDtypeStruct(x.shape, x.dtype) for x in (token, *arrays)],
        in_specs=[whole] + [place] * len(arrays),
        out_specs=[whole] * (1 + len(arrays)),
        scratch_shapes=[pltpu.SemaphoreType.DMA((len(arrays),))],
        compiler_params=pltpu.CompilerParams(vmem_limit_bytes=1 << 20),
        cost_estimate=pl.CostEstimate(flops=1, bytes_accessed=1, transcendentals=0),
        name="load",
    )(token, *arrays)


def ring_orders(devices):
    chips = devices // 2
    order = [2 * r if r < chips // 2 else 2 * (chips - 1 - r) + 1 for r in range(chips)]
    forward = [
        (2 * order[r] + core, 2 * order[(r + 1) % chips] + core)
        for r in range(chips)
        for core in range(2)
    ]
    backward = [(b, a) for a, b in forward]
    swap = [(i, i ^ 1) for i in range(devices)]
    return forward, backward, swap


def fence_kernel(token_ref, *refs):
    refs[len(refs) // 2][...] = token_ref[...]


def fence(token, values):
    place = pl.BlockSpec(memory_space=pl.ANY)
    whole = pl.BlockSpec(memory_space=pltpu.VMEM)
    token, *values = pl.pallas_call(
        fence_kernel,
        out_shape=[jax.ShapeDtypeStruct(x.shape, x.dtype) for x in (token, *values)],
        in_specs=[whole] + [place] * len(values),
        out_specs=[whole] + [place] * len(values),
        input_output_aliases={k: k for k in range(1, len(values) + 1)},
        compiler_params=pltpu.CompilerParams(vmem_limit_bytes=1 << 20),
        cost_estimate=pl.CostEstimate(flops=1, bytes_accessed=4 << 20, transcendentals=0),
        name="fence",
    )(token, *values)
    return token, values


def merge_kernel(token_ref, ahead_terms, behind_terms, *refs, cuts):
    *moving, next_ref, ahead_ref, behind_ref = refs
    next_ref[...] = token_ref[...]
    for way, (terms_ref, out_ref) in enumerate(
        ((ahead_terms, ahead_ref), (behind_terms, behind_ref))
    ):
        total = terms_ref[cuts[way]]
        if moving:
            total = (total.astype(F32) + moving[way][...].astype(F32)).astype(BF16)
        out_ref[...] = total


def merge(token, terms, cuts, moving):
    whole = pl.BlockSpec(memory_space=pltpu.VMEM)
    part = jax.ShapeDtypeStruct((cuts[0].stop - cuts[0].start, terms[0].shape[1]), BF16)
    return pl.pallas_call(
        functools.partial(merge_kernel, cuts=cuts),
        out_shape=[jax.ShapeDtypeStruct(token.shape, token.dtype), part, part],
        in_specs=[whole] * (3 + len(moving)),
        out_specs=[whole] * 3,
        compiler_params=pltpu.CompilerParams(vmem_limit_bytes=4 << 20),
        cost_estimate=pl.CostEstimate(flops=1, bytes_accessed=1, transcendentals=0),
        name="merge",
    )(token, *terms, *moving)


def finish_kernel(token_ref, terms_ref, *refs):
    *sum_refs, out_ref, rows_ref, sems = refs
    batches, tokens, model_width = rows_ref.shape
    stream_refs, sum_refs = sum_refs[:batches], sum_refs[batches:]
    half = model_width // batches
    copies = []
    for batch, stream_ref in enumerate(stream_refs):
        came = slice(batch * half, (batch + 1) * half)
        for side in range(2):
            cols = slice(side * half, (side + 1) * half)
            total = terms_ref[side * tokens : (side + 1) * tokens, came].astype(F32)
            for sum_ref in sum_refs[2 * side : 2 * side + 2]:
                total = total + sum_ref[:, came].astype(F32)
            rows_ref[batch, :, cols] = (stream_ref[:, cols] + total).astype(BF16)
        copies.append(pltpu.make_async_copy(rows_ref.at[batch], out_ref.at[batch], sems.at[batch]))
        copies[-1].start()
    for copy in copies:
        copy.wait()


def finish(token, terms, streams, sums):
    whole = pl.BlockSpec(memory_space=pltpu.VMEM)
    shape = (len(streams), *streams[0].shape)
    return pl.pallas_call(
        finish_kernel,
        out_shape=jax.ShapeDtypeStruct(shape, BF16),
        in_specs=[whole] * (2 + len(streams) + len(sums)),
        out_specs=pl.BlockSpec(memory_space=pl.ANY),
        scratch_shapes=[pltpu.VMEM(shape, BF16), pltpu.SemaphoreType.DMA((len(streams),))],
        compiler_params=pltpu.CompilerParams(vmem_limit_bytes=8 << 20),
        name="finish",
    )(token, terms, *streams, *sums)


class Line:
    def __init__(self):
        self.token = jnp.zeros((16, 128), F32)

    def hold(self, values):
        self.token, values = fence(self.token, values)
        return values


def body(queries, keys_values, residual, norm_gain, gate_up, down_proj, expert_ids, expert_gates):
    devices = lax.axis_size("dev")
    batches, tokens, model_width = residual.shape
    length, feat_width = queries.shape[2:]
    kv_heads = model_width // feat_width
    forward, backward, swap = ring_orders(devices)
    chips = devices // 2
    reach = chips // 2
    half = model_width // 2
    me = lax.axis_index("dev").astype(jnp.int32).reshape(1)
    me, queries = lax.optimization_barrier((me, queries))
    send_ahead = lambda x: lax.ppermute(x, "dev", forward)
    send_behind = lambda x: lax.ppermute(x, "dev", backward)
    swapped = lambda x: lax.ppermute(x, "dev", swap)
    line = Line()

    gate_up_b, down_b = swapped(gate_up), swapped(down_proj)
    rows = attend(queries, keys_values, expert_ids, expert_gates, devices)
    arrived = lax.all_to_all(
        rows.reshape(devices, -1, rows.shape[-1]), "dev", split_axis=0, concat_axis=0, tiled=True
    )
    arrived, gate_up_b, down_b = line.hold([arrived, gate_up_b, down_b])
    arrived = arrived.reshape(rows.shape)
    left, right, streams = prepare(arrived, residual, norm_gain, kv_heads)
    shares = arrived[:, 0, 0, feat_width:].astype(F32) + arrived[:, 0, 1, feat_width:].astype(F32)
    shares = [shares, swapped(shares)]

    class Chain:
        def __init__(self, ahead, behind):
            self.moving = [ahead, behind]

        def send(self):
            self.moving = [send_ahead(self.moving[0]), send_behind(self.moving[1])]

        def land(self):
            self.moving = line.hold(self.moving)

    long, short = Chain(left, right), Chain(right, left)
    held = {0: [left, right]}
    terms = {}

    def experts(*places):
        blocks = [block for place in places for block in held[place]]
        out, line.token = run_experts(me, line.token, shares, weights, blocks, places)
        for k, place in enumerate(places):
            terms[place] = (out, 2 * k * tokens)

    def send_back(chain, step, first=False):
        pairs = ((step, 0), (-step % chips, 1)) if chain is long else ((step, 1), (-step % chips, 0))
        outs, cuts = [], []
        for place, side in pairs:
            out, row = terms[place]
            outs.append(out)
            cuts.append(slice(row + side * tokens, row + (side + 1) * tokens))
        line.token, *chain.moving = merge(line.token, outs, cuts, [] if first else chain.moving)
        chain.send()

    long.send()
    short.send()
    line.token, gate_up_b = load(line.token, gate_up_b)
    weights = [gate_up, gate_up_b, down_proj, down_b]
    for step in range(1, reach):
        long.land()
        from_behind, from_ahead = long.moving
        long.send()
        if step == reach - 1:
            *begun, line.token = begin_experts(
                line.token, weights, [from_ahead, from_behind], (1, 0)
            )
        elif step == 2:
            experts(chips - 1)
        short.land()
        held[step] = [short.moving[1], from_ahead]
        held[chips - step] = [from_behind, short.moving[0]]
        if step < reach - 1:
            short.send()
        if step == reach - 1:
            places = (step, chips - step)
            out, line.token = run_experts(
                me, line.token, shares, weights, short.moving[::-1], places, (0, 1), begun
            )
            terms.update({place: (out, 2 * k * tokens) for k, place in enumerate(places)})
        elif step == 1:
            experts(1)
        else:
            experts(step, chips - step)
    if reach < 4:
        experts(chips - 1)
    send_back(short, reach - 1, True)
    long.land()
    held[reach] = long.moving
    experts(reach)
    send_back(long, reach, True)
    for step in range(reach - 2, 0, -1):
        send_back(short, step)
        send_back(long, step + 1)
        if step == 1:
            experts(0)
    short.land()
    send_back(long, 1)
    ahead, behind = long.moving
    short_ahead, short_behind = short.moving
    return finish(
        line.token, terms[0][0], streams, [ahead, short_behind, behind, short_ahead]
    )


def solution(mesh):
    in_specs = (
        P(None, ("groups", "dev"), None, None),
        P(None, ("groups", "dev"), None, None, None),
        P(None, ("groups", "dev"), None),
        P(),
        P("dev", None, None),
        P("dev", None, None),
        P(None, ("groups", "dev"), None),
        P(None, ("groups", "dev"), None),
    )
    out_specs = P(None, ("groups", "dev"), None)
    return jax.shard_map(body, mesh=mesh, in_specs=in_specs, out_specs=out_specs, check_vma=False)
```

```python
import functools
import math

import jax
import jax.numpy as jnp
import numpy as np
from jax import lax
from jax.experimental import pallas as pl
from jax.experimental.pallas import tpu as pltpu
from jax.sharding import PartitionSpec as P

F32 = jnp.float32
BF16 = jnp.bfloat16


def attend_kernel(q_ref, kv_ref, ids_ref, gates_ref, out_ref, values_ref, *, devices):
    length, feat_width = q_ref.shape
    context, head_size = kv_ref.shape[1:]
    positions = length // devices
    scale = math.log2(math.e) / math.sqrt(head_size)
    keys = kv_ref[0]
    values_ref[:, :head_size] = kv_ref[1]
    values_ref[:, head_size:] = jnp.ones((context, head_size), BF16)
    row = lax.broadcasted_iota(jnp.int32, (length, length), 0)
    col = lax.broadcasted_iota(jnp.int32, (length, length), 1)
    heads = feat_width // head_size
    stack = next(k for k in (4, 2, 1) if heads % k == 0)
    allowed = jnp.concatenate([col <= row] * stack, axis=0)

    def put(cols, value):
        if len(out_ref.shape) == 3:
            value = value.reshape(devices, positions, value.shape[-1])
            out_ref[:, :, cols] = value.astype(BF16)
        else:
            out_ref[:, cols] = value.astype(BF16)

    for first in range(0, heads, stack):
        cols = [slice(h * head_size, (h + 1) * head_size) for h in range(first, first + stack)]
        scores = lax.dot_general(
            jnp.concatenate([q_ref[:, c] for c in cols], axis=0),
            keys,
            (((1,), (1,)), ((), ())),
            preferred_element_type=F32,
        )
        cached = scores[:, : context - length]
        fresh = jnp.where(allowed, scores[:, context - length :], -1e30)
        highest = jnp.maximum(
            jnp.max(cached, axis=-1, keepdims=True), jnp.max(fresh, axis=-1, keepdims=True)
        )
        grown = jnp.concatenate(
            [jnp.exp2((cached - highest) * scale), jnp.exp2((fresh - highest) * scale)], axis=1
        )
        both = jnp.dot(grown.astype(BF16), values_ref[...], preferred_element_type=F32)
        blended = both[:, :head_size] / both[:, head_size:]
        for k, c in enumerate(cols):
            put(c, blended[k * length : (k + 1) * length])

    batches, top, tokens = ids_ref.shape
    lines = batches * tokens
    last = slice(feat_width, feat_width + lines)

    @pl.when(pl.program_id(0) == 0)
    def _():
        tables = []
        for batch in range(batches):
            shares = gates_ref[batch].astype(F32)
            shares = shares / jnp.sum(shares, axis=0, keepdims=True)
            expert = lax.broadcasted_iota(jnp.int32, (devices, tokens), 0)
            table = jnp.zeros((devices, tokens), F32)
            for k in range(top):
                named = expert == ids_ref[batch, k : k + 1]
                table += jnp.where(named, shares[k : k + 1], 0.0)
            tables.append(table)
        table = jnp.concatenate(tables, axis=1)
        high = table.astype(BF16).astype(F32)
        part = lax.broadcasted_iota(jnp.int32, (devices, positions, lines), 1)
        spread = [jnp.broadcast_to(x[:, None, :], part.shape) for x in (high, table - high)]
        both = jnp.where(part == 0, spread[0], jnp.where(part == 1, spread[1], 0.0))
        put(last, both.reshape(length, lines))

    @pl.when(pl.program_id(0) > 0)
    def _():
        put(last, jnp.zeros((length, lines), F32))


def attend(queries, keys_values, expert_ids, expert_gates, devices):
    batches, _, length, feat_width = queries.shape
    context, head_size = keys_values.shape[3:]
    positions = length // devices
    pairs = batches * length * (feat_width // head_size) * context
    queries, keys_values, *choices = [
        pltpu.with_memory_space_constraint(x, pltpu.HBM)
        for x in (
            queries,
            keys_values,
            jnp.swapaxes(expert_ids, 1, 2),
            jnp.swapaxes(expert_gates, 1, 2),
        )
    ]
    width = feat_width + batches * expert_ids.shape[1]
    direct = positions % 8 == 0
    if direct:
        shape = (devices, batches, positions, width)
        out_spec = pl.BlockSpec((devices, None, positions, width), lambda i: (0, i, 0, 0))
    else:
        shape = (batches, length, width)
        out_spec = pl.BlockSpec((None, length, width), lambda i: (i, 0, 0))
    rows = pl.pallas_call(
        functools.partial(attend_kernel, devices=devices),
        out_shape=jax.ShapeDtypeStruct(shape, BF16),
        grid=(batches,),
        in_specs=[
            pl.BlockSpec((None, None, length, feat_width), lambda i: (i, 0, 0, 0)),
            pl.BlockSpec((None, None, 2, context, head_size), lambda i: (i, 0, 0, 0, 0)),
        ]
        + [pl.BlockSpec(c.shape, lambda i: (0, 0, 0)) for c in choices],
        out_specs=out_spec,
        scratch_shapes=[pltpu.VMEM((context, 2 * head_size), BF16)],
        compiler_params=pltpu.CompilerParams(vmem_limit_bytes=14 << 20),
        cost_estimate=pl.CostEstimate(
            flops=4 * pairs * head_size,
            bytes_accessed=2 * batches * (2 * length * feat_width + 2 * context * head_size),
            transcendentals=pairs,
        ),
        name="attend",
    )(queries, keys_values, *choices)
    if not direct:
        rows = jnp.swapaxes(rows.reshape(batches, devices, positions, width), 0, 1)
    return rows


def prepare_kernel(arrived_ref, residual_ref, gain_ref, left_ref, right_ref, *stream_refs, kv_heads):
    batches, tokens, model_width = residual_ref.shape
    feat_width = model_width // kv_heads
    half = model_width // batches
    for batch, stream_ref in enumerate(stream_refs):
        if len(arrived_ref.shape) == 4:
            sources, _, positions, _ = arrived_ref.shape
            for source in range(sources):
                first = source // kv_heads * positions
                left = source % kv_heads * feat_width
                stream_ref[first : first + positions, left : left + feat_width] = arrived_ref[
                    source, batch, :, :feat_width
                ].astype(F32)
            rows = stream_ref[...]
        else:
            rows = arrived_ref[batch].astype(F32)
        stream = residual_ref[batch].astype(F32) + rows
        stream_ref[...] = stream
        meansq = jnp.mean(stream * stream, axis=-1, keepdims=True)
        own = (stream * lax.rsqrt(meansq + 1e-06) * gain_ref[...]).astype(BF16)
        left_ref[:, batch * half : (batch + 1) * half] = own[:, :half]
        right_ref[:, batch * half : (batch + 1) * half] = own[:, half:]


def prepare(arrived, residual, norm_gain, kv_heads):
    batches, tokens, model_width = residual.shape
    sources, _, positions, _ = arrived.shape
    feat_width = model_width // kv_heads
    if positions % 8:
        rows = arrived[..., :feat_width]
        rows = rows.reshape(sources // kv_heads, kv_heads, batches, positions, feat_width)
        arrived = jnp.transpose(rows, (2, 0, 3, 1, 4)).reshape(batches, tokens, model_width)
    row = (tokens, model_width)
    whole = pl.BlockSpec(memory_space=pltpu.VMEM)
    left, right, *streams = pl.pallas_call(
        functools.partial(prepare_kernel, kv_heads=kv_heads),
        out_shape=[jax.ShapeDtypeStruct(row, BF16)] * 2
        + [jax.ShapeDtypeStruct(row, F32)] * batches,
        in_specs=[whole] * 3,
        out_specs=[whole] * (2 + batches),
        compiler_params=pltpu.CompilerParams(vmem_limit_bytes=4 << 20),
        name="prepare",
    )(arrived, residual, norm_gain.reshape(1, model_width))
    return left, right, streams


def ring_place(device, step, devices):
    chips = devices // 2
    chip, core = device // 2, device % 2
    place = jnp.where(chip % 2 == 0, chip // 2, chips - 1 - chip // 2)
    place = (place + step) % chips
    chip = jnp.where(place < chips // 2, 2 * place, 2 * (chips - 1 - place) + 1)
    return 2 * chip + core


def pre_activations(x_ref, gate_up_ref, cols, sides, blocks):
    if sides is None:
        return jnp.dot(x_ref[...], gate_up_ref[0, :, cols], preferred_element_type=F32)
    rows, half = x_ref.shape
    rows = rows // blocks
    parts = []
    for block, side in enumerate(sides):
        parts.append(
            jnp.dot(
                x_ref[block * rows : (block + 1) * rows],
                gate_up_ref[0, side * half : (side + 1) * half, cols],
                preferred_element_type=F32,
            )
        )
    return jnp.concatenate(parts, axis=0)


def gather_halves(x_ref, half_refs):
    tokens, width = half_refs[0].shape
    for block, ref in enumerate(half_refs):
        for batch in range(2):
            row = (2 * block + batch) * tokens
            came = slice(batch * width // 2, (batch + 1) * width // 2)
            x_ref[row : row + tokens] = ref[:, came]


def begin_kernel(token_ref, gate_up_a, gate_up_b, *refs, sides):
    *half_refs, pre_a, pre_b, next_ref, x_ref = refs
    next_ref[...] = token_ref[...]
    gather_halves(x_ref, half_refs)
    for gate_up_ref, pre_ref in ((gate_up_a, pre_a), (gate_up_b, pre_b)):
        width = pre_ref.shape[1]
        part = min(256, width)
        for start in range(0, width, part):
            cols = slice(start, start + part)
            pre_ref[:, cols] = pre_activations(x_ref, gate_up_ref, cols, sides, len(half_refs))


def begin_experts(token, weights, halves, sides):
    tokens, width = halves[0].shape
    rows = 2 * tokens * len(halves)
    hidden = weights[0].shape[2]
    whole = pl.BlockSpec(memory_space=pltpu.VMEM)
    return pl.pallas_call(
        functools.partial(begin_kernel, sides=sides),
        out_shape=[jax.ShapeDtypeStruct((rows, hidden), F32)] * 2
        + [jax.ShapeDtypeStruct(token.shape, token.dtype)],
        in_specs=[whole] * (3 + len(halves)),
        out_specs=[whole] * 3,
        scratch_shapes=[pltpu.VMEM((rows, width // 2), BF16)],
        compiler_params=pltpu.CompilerParams(vmem_limit_bytes=4 << 20),
        cost_estimate=pl.CostEstimate(flops=1, bytes_accessed=1, transcendentals=0),
        name="begin",
    )(token, *weights[:2], *halves)


def expert_kernel(
    me_ref, token_ref, share_a, share_b, gate_up_a, gate_up_b, down_a, down_b, *refs, places, sides
):
    *held_refs, out_ref, next_ref, x_all, hidden_a, hidden_b = refs
    next_ref[...] = token_ref[...]
    begun = (None, None)
    if sides is not None:
        *held_refs, pre_a, pre_b = held_refs
        begun = (pre_a, pre_b)
    tokens, model_width = held_refs[0].shape
    half = model_width // 2
    blocks = len(places)
    hidden_width = down_a.shape[1]
    devices, lanes = share_a.shape
    part = min(256, hidden_width)
    chunk = min(512, half)

    row_of = lambda block, batch: (block * 2 + batch) * tokens
    if sides is not None:
        gather_halves(x_all, held_refs)
    else:
        for block in range(blocks):
            for side in range(2):
                cols = slice(side * half, (side + 1) * half)
                for batch in range(2):
                    row = row_of(block, batch)
                    came = slice(batch * half, (batch + 1) * half)
                    x_all[row : row + tokens, cols] = held_refs[2 * block + side][:, came]
    token = lax.broadcasted_iota(jnp.int32, (tokens, lanes), 0)
    lane = lax.broadcasted_iota(jnp.int32, (tokens, lanes), 1)
    for share_ref, gate_up_ref, hidden_ref, pre_ref in (
        (share_a, gate_up_a, hidden_a, begun[0]),
        (share_b, gate_up_b, hidden_b, begun[1]),
    ):
        shares = []
        for place in places:
            source = ring_place(me_ref[0], place, devices)
            line = jnp.broadcast_to(share_ref[pl.ds(source, 1), :], (tokens, lanes))
            for batch in range(2):
                spread = jnp.where(lane == token + batch * tokens, line, 0.0)
                shares.append(jnp.sum(spread, axis=-1, keepdims=True))
        share = jnp.concatenate(shares, axis=0)
        for start in range(0, hidden_width, part):
            pair = []
            for first in (start, hidden_width + start):
                cols = slice(first, first + part)
                pre = pre_activations(x_all, gate_up_ref, cols, sides, blocks)
                pair.append(pre if pre_ref is None else pre + pre_ref[:, cols])
            gate, up = pair
            act = gate / (1.0 + jnp.exp(-gate)) * up
            hidden_ref[:, start : start + part] = (act * share).astype(BF16)
    for start in range(0, model_width, chunk):
        cols = slice(start, start + chunk)
        total = jnp.dot(hidden_a[...], down_a[0, :, cols], preferred_element_type=F32)
        total += jnp.dot(hidden_b[...], down_b[0, :, cols], preferred_element_type=F32)
        weighted = total.astype(BF16)
        side, left = start // half, start % half
        for block in range(blocks):
            rows = slice((2 * block + side) * tokens, (2 * block + side + 1) * tokens)
            for batch in range(2):
                row = row_of(block, batch)
                goes = slice(batch * half + left, batch * half + left + chunk)
                out_ref[rows, goes] = weighted[row : row + tokens]


def run_experts(me, token, shares, weights, held, places, sides=None, begun=()):
    tokens, model_width = held[0].shape
    rows = 2 * tokens * len(places)
    hidden_width = weights[2].shape[1]
    whole = pl.BlockSpec(memory_space=pltpu.VMEM)
    return pl.pallas_call(
        functools.partial(expert_kernel, places=places, sides=sides),
        out_shape=[
            jax.ShapeDtypeStruct((rows, model_width), BF16),
            jax.ShapeDtypeStruct(token.shape, token.dtype),
        ],
        in_specs=[pl.BlockSpec(memory_space=pltpu.SMEM)] + [whole] * (7 + len(held) + len(begun)),
        out_specs=[whole] * 2,
        scratch_shapes=[
            pltpu.VMEM((rows, model_width if sides is None else model_width // 2), BF16),
            pltpu.VMEM((rows, hidden_width), BF16),
            pltpu.VMEM((rows, hidden_width), BF16),
        ],
        compiler_params=pltpu.CompilerParams(vmem_limit_bytes=6 << 20),
        cost_estimate=pl.CostEstimate(flops=1, bytes_accessed=1, transcendentals=0),
        name="experts",
    )(me, token, *shares, *weights, *held, *begun)


def load_kernel(token_ref, *refs):
    count = len(refs) // 2 - 1
    next_ref, *out_refs = refs[count:-1]
    copies = [
        pltpu.make_async_copy(ref, out_ref, refs[-1].at[k])
        for k, (ref, out_ref) in enumerate(zip(refs[:count], out_refs))
    ]
    for copy in copies:
        copy.start()
    next_ref[...] = token_ref[...]
    for copy in copies:
        copy.wait()


def load(token, *arrays):
    whole = pl.BlockSpec(memory_space=pltpu.VMEM)
    place = pl.BlockSpec(memory_space=pl.ANY)
    return pl.pallas_call(
        load_kernel,
        out_shape=[jax.ShapeDtypeStruct(x.shape, x.dtype) for x in (token, *arrays)],
        in_specs=[whole] + [place] * len(arrays),
        out_specs=[whole] * (1 + len(arrays)),
        scratch_shapes=[pltpu.SemaphoreType.DMA((len(arrays),))],
        compiler_params=pltpu.CompilerParams(vmem_limit_bytes=1 << 20),
        cost_estimate=pl.CostEstimate(flops=1, bytes_accessed=1, transcendentals=0),
        name="load",
    )(token, *arrays)


def ring_orders(devices):
    chips = devices // 2
    order = [2 * r if r < chips // 2 else 2 * (chips - 1 - r) + 1 for r in range(chips)]
    forward = [
        (2 * order[r] + core, 2 * order[(r + 1) % chips] + core)
        for r in range(chips)
        for core in range(2)
    ]
    backward = [(b, a) for a, b in forward]
    swap = [(i, i ^ 1) for i in range(devices)]
    return forward, backward, swap


def fence_kernel(token_ref, *refs):
    refs[len(refs) // 2][...] = token_ref[...]


def fence(token, values):
    place = pl.BlockSpec(memory_space=pl.ANY)
    whole = pl.BlockSpec(memory_space=pltpu.VMEM)
    token, *values = pl.pallas_call(
        fence_kernel,
        out_shape=[jax.ShapeDtypeStruct(x.shape, x.dtype) for x in (token, *values)],
        in_specs=[whole] + [place] * len(values),
        out_specs=[whole] + [place] * len(values),
        input_output_aliases={k: k for k in range(1, len(values) + 1)},
        compiler_params=pltpu.CompilerParams(vmem_limit_bytes=1 << 20),
        cost_estimate=pl.CostEstimate(flops=1, bytes_accessed=4 << 20, transcendentals=0),
        name="fence",
    )(token, *values)
    return token, values


def merge_kernel(token_ref, ahead_terms, behind_terms, *refs, cuts):
    *moving, next_ref, ahead_ref, behind_ref = refs
    next_ref[...] = token_ref[...]
    for way, (terms_ref, out_ref) in enumerate(
        ((ahead_terms, ahead_ref), (behind_terms, behind_ref))
    ):
        total = terms_ref[cuts[way]]
        if moving:
            total = (total.astype(F32) + moving[way][...].astype(F32)).astype(BF16)
        out_ref[...] = total


def merge(token, terms, cuts, moving):
    whole = pl.BlockSpec(memory_space=pltpu.VMEM)
    part = jax.ShapeDtypeStruct((cuts[0].stop - cuts[0].start, terms[0].shape[1]), BF16)
    return pl.pallas_call(
        functools.partial(merge_kernel, cuts=cuts),
        out_shape=[jax.ShapeDtypeStruct(token.shape, token.dtype), part, part],
        in_specs=[whole] * (3 + len(moving)),
        out_specs=[whole] * 3,
        compiler_params=pltpu.CompilerParams(vmem_limit_bytes=2 << 20),
        cost_estimate=pl.CostEstimate(flops=1, bytes_accessed=1, transcendentals=0),
        name="merge",
    )(token, *terms, *moving)


def finish_kernel(token_ref, terms_ref, *refs):
    *sum_refs, out_ref, rows_ref, sems = refs
    batches, tokens, model_width = rows_ref.shape
    stream_refs, sum_refs = sum_refs[:batches], sum_refs[batches:]
    half = model_width // batches
    copies = []
    for batch, stream_ref in enumerate(stream_refs):
        came = slice(batch * half, (batch + 1) * half)
        for side in range(2):
            cols = slice(side * half, (side + 1) * half)
            total = terms_ref[side * tokens : (side + 1) * tokens, came].astype(F32)
            for sum_ref in sum_refs[2 * side : 2 * side + 2]:
                total = total + sum_ref[:, came].astype(F32)
            rows_ref[batch, :, cols] = (stream_ref[:, cols] + total).astype(BF16)
        copies.append(pltpu.make_async_copy(rows_ref.at[batch], out_ref.at[batch], sems.at[batch]))
        copies[-1].start()
    for copy in copies:
        copy.wait()


def finish(token, terms, streams, sums):
    whole = pl.BlockSpec(memory_space=pltpu.VMEM)
    shape = (len(streams), *streams[0].shape)
    return pl.pallas_call(
        finish_kernel,
        out_shape=jax.ShapeDtypeStruct(shape, BF16),
        in_specs=[whole] * (2 + len(streams) + len(sums)),
        out_specs=pl.BlockSpec(memory_space=pl.ANY),
        scratch_shapes=[pltpu.VMEM(shape, BF16), pltpu.SemaphoreType.DMA((len(streams),))],
        compiler_params=pltpu.CompilerParams(vmem_limit_bytes=4 << 20),
        name="finish",
    )(token, terms, *streams, *sums)


class Line:
    def __init__(self):
        self.token = jnp.zeros((16, 128), F32)

    def hold(self, values):
        self.token, values = fence(self.token, values)
        return values


def body(queries, keys_values, residual, norm_gain, gate_up, down_proj, expert_ids, expert_gates):
    devices = lax.axis_size("dev")
    batches, tokens, model_width = residual.shape
    length, feat_width = queries.shape[2:]
    kv_heads = model_width // feat_width
    forward, backward, swap = ring_orders(devices)
    chips = devices // 2
    reach = chips // 2
    half = model_width // 2
    me = lax.axis_index("dev").astype(jnp.int32).reshape(1)
    me, queries = lax.optimization_barrier((me, queries))
    send_ahead = lambda x: lax.ppermute(x, "dev", forward)
    send_behind = lambda x: lax.ppermute(x, "dev", backward)
    swapped = lambda x: lax.ppermute(x, "dev", swap)
    line = Line()

    gate_up_b, down_b = swapped(gate_up), swapped(down_proj)
    rows = attend(queries, keys_values, expert_ids, expert_gates, devices)
    arrived = lax.all_to_all(
        rows.reshape(devices, -1, rows.shape[-1]), "dev", split_axis=0, concat_axis=0, tiled=True
    )
    arrived, gate_up_b, down_b = line.hold([arrived, gate_up_b, down_b])
    arrived = arrived.reshape(rows.shape)
    left, right, streams = prepare(arrived, residual, norm_gain, kv_heads)
    shares = arrived[:, 0, 0, feat_width:].astype(F32) + arrived[:, 0, 1, feat_width:].astype(F32)
    shares = [shares, swapped(shares)]

    class Chain:
        def __init__(self, ahead, behind):
            self.moving = [ahead, behind]

        def send(self):
            self.moving = [send_ahead(self.moving[0]), send_behind(self.moving[1])]

        def land(self):
            self.moving = line.hold(self.moving)

    long, short = Chain(left, right), Chain(right, left)
    held = {0: [left, right]}
    terms = {}

    def experts(*places):
        blocks = [block for place in places for block in held[place]]
        out, line.token = run_experts(me, line.token, shares, weights, blocks, places)
        for k, place in enumerate(places):
            terms[place] = (out, 2 * k * tokens)

    def send_back(chain, step, first=False):
        pairs = ((step, 0), (-step % chips, 1)) if chain is long else ((step, 1), (-step % chips, 0))
        outs, cuts = [], []
        for place, side in pairs:
            out, row = terms[place]
            outs.append(out)
            cuts.append(slice(row + side * tokens, row + (side + 1) * tokens))
        line.token, *chain.moving = merge(line.token, outs, cuts, [] if first else chain.moving)
        chain.send()

    long.send()
    short.send()
    line.token, gate_up_b = load(line.token, gate_up_b)
    weights = [gate_up, gate_up_b, down_proj, down_b]
    for step in range(1, reach):
        long.land()
        from_behind, from_ahead = long.moving
        long.send()
        if step == reach - 1:
            *begun, line.token = begin_experts(
                line.token, weights, [from_ahead, from_behind], (1, 0)
            )
        elif step == 2:
            experts(chips - 1)
        short.land()
        held[step] = [short.moving[1], from_ahead]
        held[chips - step] = [from_behind, short.moving[0]]
        if step < reach - 1:
            short.send()
        if step == reach - 1:
            places = (step, chips - step)
            out, line.token = run_experts(
                me, line.token, shares, weights, short.moving[::-1], places, (0, 1), begun
            )
            terms.update({place: (out, 2 * k * tokens) for k, place in enumerate(places)})
        elif step == 1:
            experts(1)
        else:
            experts(step, chips - step)
    if reach < 4:
        experts(chips - 1)
    send_back(short, reach - 1, True)
    long.land()
    held[reach] = long.moving
    experts(reach)
    send_back(long, reach, True)
    for step in range(reach - 2, 0, -1):
        send_back(short, step)
        send_back(long, step + 1)
        if step == 1:
            experts(0)
    short.land()
    send_back(long, 1)
    ahead, behind = long.moving
    short_ahead, short_behind = short.moving
    return finish(
        line.token, terms[0][0], streams, [ahead, short_behind, behind, short_ahead]
    )


def solution(mesh):
    in_specs = (
        P(None, ("groups", "dev"), None, None),
        P(None, ("groups", "dev"), None, None, None),
        P(None, ("groups", "dev"), None),
        P(),
        P("dev", None, None),
        P("dev", None, None),
        P(None, ("groups", "dev"), None),
        P(None, ("groups", "dev"), None),
    )
    out_specs = P(None, ("groups", "dev"), None)
    return jax.shard_map(body, mesh=mesh, in_specs=in_specs, out_specs=out_specs, check_vma=False)
```
